256 devices in a mesh: phase: 4 (over x), dom: 64 (over y, z, core).
Axes of the slice: x: 4, y: 4, z: 8, core: 2. Of those that a mesh axis runs over, the one named last changes fastest.
Arguments:
- edges_fwd: bfloat16 [4, 49152, 256], P('phase', 'dom'), may hold values from -6 to 6
- nodes_fwd: bfloat16 [4, 65536, 256], P('phase', 'dom'), may hold values from -6 to 6
- edges_stash: bfloat16 [4, 49152, 256], P('phase', 'dom'), may hold values from -6 to 6
- nodes_stash: bfloat16 [4, 65536, 256], P('phase', 'dom'), may hold values from -6 to 6
- edge_cot: bfloat16 [4, 49152, 256], P('phase', 'dom'), may hold values from -6 to 6
- node_cot: bfloat16 [4, 65536, 256], P('phase', 'dom'), may hold values from -6 to 6
- edge_w1: bfloat16 [4, 768, 256], P('phase'), may hold values from -0.21875 to 0.21875
- edge_w2: bfloat16 [4, 256, 256], P('phase'), may hold values from -0.375 to 0.375
- edge_vectors: float32 [4, 4, 256], P('phase'), may hold values from -2 to 2
- node_w1: bfloat16 [4, 512, 256], P('phase'), may hold values from -0.25 to 0.25
- node_w2: bfloat16 [4, 256, 256], P('phase'), may hold values from -0.375 to 0.375
- node_vectors: float32 [4, 4, 256], P('phase'), may hold values from -2 to 2
- edge_nodes: int32 [2, 49152], P(None, 'dom'), may hold values from 0 to 1535, as said below
- mirror_rows: int32 [64, 64, 8], P('dom'), may hold values from 0 to 1023
- edge_count: int32 [64], P('dom'), may hold values from 1 to 768, 30720 in all
Outputs:
- next_edges: bfloat16 [4, 49152, 256], P('phase', 'dom')
- next_nodes: bfloat16 [4, 65536, 256], P('phase', 'dom')
- prev_edge_grads: bfloat16 [4, 49152, 256], P('phase', 'dom')
- prev_node_grads: bfloat16 [4, 65536, 256], P('phase', 'dom')
- grad_edge_w1: float32 [4, 768, 256], P('phase')
- grad_edge_w2: float32 [4, 256, 256], P('phase')
- grad_edge_vectors: float32 [4, 4, 256], P('phase')
- grad_node_w1: float32 [4, 512, 256], P('phase')
- grad_node_w2: float32 [4, 256, 256], P('phase')
- grad_node_vectors: float32 [4, 4, 256], P('phase')
The draws below stay inside these ranges and needn't reach their ends.
Inputs may be any that keep to these rules, and one draw needn't show every extreme that they name: `edge_nodes`: columns d * 768 to (d + 1) * 768 - 1 belong to dom index d and name rows of its node table. In each aligned block of 128 edge slots, all receivers lie in one tile of 128 table rows and all senders in one tile. `mirror_rows`: entry [p, d, c] is the row of owner p's nodes that dom index d holds as its mirrored row c of owner p. The live edges of dom index d are its first edge_count[d] edge slots.
All inputs are finite; a program needn't handle non-finite values. No bound on the sum of `edge_count` on one device may be relied on, other than what follows from the above.
Results may differ from the reference program's by a relative error of at most 0.024.
The reference program's roundings to bfloat16 on the way count: a program that leaves them out, or rounds other values in their place, can miss the bound.
Values may be sent and summed in bfloat16 or wider, within the bound.
A program may use at most 64 MiB of HBM per device.

```python
import math
import jax
import jax.numpy as jnp
import numpy as np
from jax import lax

D = 256
TILE = 128
NODE_DEV = 1024
EDGE_DEV = 768
MIRROR_DEV = 512
CAP = 8
SLOT_ROWS = 1536
NODES = 65536
EDGES = 49152
LIVE_EDGES = 30720
N_PHASE = 4
N_DOM = 64


def draw_edge_nodes(key, part):
    block_count = EDGES // TILE
    tile_count = SLOT_ROWS // TILE
    sender_key, receiver_key, sender_row_key, receiver_row_key = jax.random.split(key, 4)
    sender_tile = jax.random.randint(sender_key, (block_count, 1), 0, tile_count)
    receiver_tile = jax.random.randint(receiver_key, (block_count, 1), 0, tile_count)
    sender_rows = jax.random.randint(sender_row_key, (block_count, TILE), 0, TILE)
    receiver_rows = jax.random.randint(receiver_row_key, (block_count, TILE), 0, TILE)
    senders = (sender_tile * TILE + sender_rows).reshape(EDGES)
    receivers = (receiver_tile * TILE + receiver_rows).reshape(EDGES)
    return jnp.stack([senders, receivers]).astype(jnp.int32)


def vector_rows(key):
    spread_key, gain_key = jax.random.split(key)
    spread = jnp.clip(0.5 * jax.random.normal(spread_key, (N_PHASE, 4, D), jnp.float32), -2.0, 2.0)
    gains = 1.0 + jax.random.uniform(gain_key, (N_PHASE, 4, D), jnp.float32, -0.17, 0.17)
    is_gain = (jnp.arange(4) == 2)[None, :, None]
    return jnp.where(is_gain, gains, spread).astype(jnp.float32)


def draw_edge_vectors(key, part):
    return vector_rows(jax.random.fold_in(key, 11))


def draw_node_vectors(key, part):
    return vector_rows(jax.random.fold_in(key, 23))


def touch_ends(array, own_key, least, top_value):
    spot = [jax.random.randint(jax.random.fold_in(own_key, axis), (), 0, length) for axis, length in enumerate(array.shape)]
    widest = array.shape.index(max(array.shape))
    next_to = spot[:widest] + [(spot[widest] + 1) % array.shape[widest]] + spot[widest + 1:]
    return array.at[tuple(spot)].set(least).at[tuple(next_to)].set(top_value)


def shard_levels(rng, shape, cuts, low, high):
    level, own = 1.0, jax.random.fold_in(rng, 6)
    for axis_at, shards_of in cuts:
        draws = jnp.exp(jax.random.uniform(jax.random.fold_in(own, axis_at), (shards_of,), jnp.float32, low / len(cuts), high / len(cuts)))
        level = level * jnp.repeat(draws, shape[axis_at] // shards_of).reshape([-1 if axis == axis_at else 1 for axis in range(len(shape))])
    return level


def length_profile(count, total, reach, slope):
    loads = [(1 << 20) // math.isqrt(rank ** slope) + 1 for rank in range(2, count + 1)]
    surplus, counts = total - reach - (count - 1), [1] * (count - 1)
    while surplus > 0:
        movable = [i for i in range(count - 1) if counts[i] < reach]
        pool, remaining = sum([loads[i] for i in movable]), surplus
        for i in movable:
            extra = min(reach - counts[i], max(1, remaining * loads[i] // pool), surplus)
            counts[i] = counts[i] + extra
            surplus = surplus - extra
    return np.array([reach] + counts)


def ragged_sizes(key, count, total, bound, lean):
    if count == 2:
        one = jax.random.randint(key, (), max(1, total - bound), min(bound, total - 1) + 1)
        return jnp.stack([one, total - one])
    sizes = jnp.asarray(length_profile(count, total, bound, lean), jnp.int32)
    pairs = (count - 1) // 2
    donor, sink = sizes[1:1 + 2 * pairs:2], sizes[2:2 + 2 * pairs:2]
    room = jnp.minimum(donor - 1, bound - sink)
    shifted = jax.random.randint(jax.random.fold_in(key, 1), (pairs,), 0, 1 << 20) % (room + 1)
    sizes = sizes.at[1:1 + 2 * pairs:2].set(donor - shifted).at[2:2 + 2 * pairs:2].set(sink + shifted)
    return sizes[jax.random.permutation(jax.random.fold_in(key, 2), count)]


def bell_draw(own_key, shape, scale, bound, shards=(), kind=jnp.bfloat16):
    values = scale * jax.random.normal(own_key, shape, jnp.float32)
    if shards:
        values = values * shard_levels(own_key, shape, shards, -0.22, 0.18)
    return jnp.clip(values, -bound, bound).astype(kind)


def setup_inputs(seed: int = 0) -> dict:
    splits = jax.random.split(jax.random.key(seed), 16)
    edges_fwd = bell_draw(splits[0], (N_PHASE, EDGES, D), 1.0, 6.0, ((0, 4), (1, 64)))
    nodes_fwd = bell_draw(splits[1], (N_PHASE, NODES, D), 1.0, 6.0, ((0, 4), (1, 64)))
    edges_stash = bell_draw(splits[2], (N_PHASE, EDGES, D), 1.0, 6.0, ((0, 4), (1, 64)))
    nodes_stash = bell_draw(splits[3], (N_PHASE, NODES, D), 1.0, 6.0, ((0, 4), (1, 64)))
    edge_cot = bell_draw(splits[4], (N_PHASE, EDGES, D), 1.0, 6.0, ((0, 4), (1, 64)))
    node_cot = bell_draw(splits[5], (N_PHASE, NODES, D), 1.0, 6.0, ((0, 4), (1, 64)))
    edge_w1 = bell_draw(splits[6], (N_PHASE, 3 * D, D), (3 * D) ** -0.5, 0.21875, ((0, 4),))
    edge_w2 = bell_draw(splits[7], (N_PHASE, D, D), D ** -0.5, 0.375, ((0, 4),))
    edge_vectors = draw_edge_vectors(jax.random.fold_in(splits[15], 71), 0)
    node_w1 = bell_draw(splits[9], (N_PHASE, 2 * D, D), (2 * D) ** -0.5, 0.25, ((0, 4),))
    node_w2 = bell_draw(splits[10], (N_PHASE, D, D), D ** -0.5, 0.375, ((0, 4),))
    node_vectors = draw_node_vectors(jax.random.fold_in(splits[15], 71), 0)
    edge_nodes = draw_edge_nodes(jax.random.fold_in(splits[15], 71), 0)
    mirror_rows = touch_ends(jax.random.randint(splits[13], (N_DOM, N_DOM, CAP), 0, NODE_DEV), jax.random.fold_in(splits[13], 1), 0, NODE_DEV - 1).astype(jnp.int32)
    edge_count = ragged_sizes(splits[14], N_DOM, LIVE_EDGES, EDGE_DEV, 2).astype(jnp.int32)
    return dict(edges_fwd=edges_fwd, nodes_fwd=nodes_fwd, edges_stash=edges_stash, nodes_stash=nodes_stash, edge_cot=edge_cot, node_cot=node_cot, edge_w1=edge_w1, edge_w2=edge_w2, edge_vectors=edge_vectors, node_w1=node_w1, node_w2=node_w2, node_vectors=node_vectors, edge_nodes=edge_nodes, mirror_rows=mirror_rows, edge_count=edge_count)


EPSILON = 1e-05

def layer_norm(pre_norm, norm_gain, norm_shift):
    row_mean = lax.optimization_barrier(jnp.mean(pre_norm, axis=-1, keepdims=True))
    centered = pre_norm - row_mean
    row_var = lax.optimization_barrier(jnp.mean(centered * centered, axis=-1, keepdims=True))
    inverse = lax.rsqrt(row_var + EPSILON)
    normed = centered * inverse
    return (normed * norm_gain + norm_shift, normed, inverse)

def norm_back(grad_out, normed, inverse, norm_gain):
    scaled = grad_out * norm_gain
    mean_first = lax.optimization_barrier(jnp.mean(scaled, axis=-1, keepdims=True))
    mean_second = lax.optimization_barrier(jnp.mean(scaled * normed, axis=-1, keepdims=True))
    return inverse * (scaled - mean_first - normed * mean_second)

def mlp_forward(stacked, first_weight, second_weight, vectors):
    pre_hidden = jnp.dot(stacked, first_weight, preferred_element_type=jnp.float32) + vectors[0]
    hidden = jnp.maximum(pre_hidden, 0.0).astype(jnp.bfloat16)
    pre_norm = jnp.dot(hidden, second_weight, preferred_element_type=jnp.float32) + vectors[1]
    normed_out, normed, inverse = layer_norm(pre_norm, vectors[2], vectors[3])
    return (normed_out, (stacked, pre_hidden, hidden, normed, inverse))

def mlp_back(grad_out, saved_rows, first_weight, second_weight, vectors):
    stacked, pre_hidden, hidden, normed, inverse = saved_rows
    gain_grad = lax.optimization_barrier(jnp.sum(grad_out * normed, axis=0))
    shift_grad = lax.optimization_barrier(jnp.sum(grad_out, axis=0))
    pre_norm_grad = norm_back(grad_out, normed, inverse, vectors[2]).astype(jnp.bfloat16)
    second_grad = jnp.dot(hidden.T, pre_norm_grad, preferred_element_type=jnp.float32)
    hidden_grad = jnp.dot(pre_norm_grad, second_weight.T, preferred_element_type=jnp.float32)
    first_pre_grad = jnp.where(pre_hidden > 0.0, hidden_grad, 0.0).astype(jnp.bfloat16)
    first_grad = jnp.dot(stacked.T, first_pre_grad, preferred_element_type=jnp.float32)
    input_grad = jnp.dot(first_pre_grad, first_weight.T, preferred_element_type=jnp.float32)
    vector_grad = jnp.stack([lax.optimization_barrier(jnp.sum(first_pre_grad.astype(jnp.float32), axis=0)), lax.optimization_barrier(jnp.sum(pre_norm_grad.astype(jnp.float32), axis=0)), gain_grad, shift_grad])
    return (input_grad, first_grad, second_grad, vector_grad)

def build_table(mirror_rows):
    owners = jnp.arange(N_DOM, dtype=jnp.int32)
    mirrored = jnp.transpose(mirror_rows, (1, 0, 2)).astype(jnp.int32) + (owners * NODE_DEV)[None, :, None]
    mirrored = mirrored.reshape(N_DOM, MIRROR_DEV)
    own_rows = owners[:, None] * NODE_DEV + jnp.arange(NODE_DEV, dtype=jnp.int32)[None, :]
    return jnp.concatenate([own_rows, mirrored], axis=1)

def home_sums(slot_sums, slot_table):
    grouped = slot_sums.reshape(N_DOM, SLOT_ROWS, D)
    own_rows = grouped[:, :NODE_DEV].reshape(NODES, D)
    mirrored = lax.optimization_barrier(grouped[:, NODE_DEV:].astype(jnp.bfloat16)).astype(jnp.float32)
    return own_rows + jax.ops.segment_sum(mirrored.reshape(N_DOM * MIRROR_DEV, D), slot_table[:, NODE_DEV:].reshape(-1), num_segments=NODES)

def forward(edges, nodes, layer, graph):
    edge_first, edge_second, edge_vec, node_first, node_second, node_vec = layer
    slot_table, slot_keys, endpoints, live_mask = graph
    stacked = jnp.concatenate([edges, nodes[endpoints[0]], nodes[endpoints[1]]], axis=1)
    normed_out, edge_saved = mlp_forward(stacked, edge_first, edge_second, edge_vec)
    message = live_mask * normed_out
    edges_new = (edges.astype(jnp.float32) + message).astype(jnp.bfloat16)
    slot_sums = jax.ops.segment_sum(message, slot_keys[1], num_segments=N_DOM * SLOT_ROWS)
    aggregate = home_sums(slot_sums, slot_table)
    node_input = jnp.concatenate([nodes, aggregate.astype(jnp.bfloat16)], axis=1)
    node_out, node_saved = mlp_forward(node_input, node_first, node_second, node_vec)
    nodes_new = (nodes.astype(jnp.float32) + node_out).astype(jnp.bfloat16)
    return (edges_new, nodes_new, edge_saved, node_saved)

def backward(edges, nodes, edge_top, node_top, layer, graph):
    edge_first, edge_second, edge_vec, node_first, node_second, node_vec = layer
    slot_table, slot_keys, endpoints, live_mask = graph
    unused_edges, unused_nodes, edge_saved, node_saved = forward(edges, nodes, layer, graph)
    node_grad_in, grad_nf, grad_ns, grad_nv = mlp_back(node_top.astype(jnp.float32), node_saved, node_first, node_second, node_vec)
    aggregate_grad = node_grad_in[:, D:].astype(jnp.bfloat16)
    edge_grad_out = live_mask * (edge_top.astype(jnp.float32) + aggregate_grad[endpoints[1]].astype(jnp.float32))
    edge_grad_in, grad_ef, grad_es, grad_ev = mlp_back(edge_grad_out, edge_saved, edge_first, edge_second, edge_vec)
    edges_grad = (edge_top.astype(jnp.float32) + edge_grad_in[:, :D]).astype(jnp.bfloat16)
    grad_terms = jnp.concatenate([edge_grad_in[:, D:2 * D], edge_grad_in[:, 2 * D:]], axis=0)
    grad_keys = jnp.concatenate([slot_keys[0], slot_keys[1]])
    slot_sums = jax.ops.segment_sum(grad_terms, grad_keys, num_segments=N_DOM * SLOT_ROWS)
    nodes_grad = (node_top.astype(jnp.float32) + node_grad_in[:, :D] + home_sums(slot_sums, slot_table)).astype(jnp.bfloat16)
    return (edges_grad, nodes_grad, (grad_ef, grad_es, grad_ev, grad_nf, grad_ns, grad_nv))

def reference(edges_fwd, nodes_fwd, edges_stash, nodes_stash, edge_cot, node_cot, edge_w1, edge_w2, edge_vectors, node_w1, node_w2, node_vectors, edge_nodes, mirror_rows, edge_count):
    slot_table = build_table(mirror_rows)
    device_of = jnp.arange(EDGES, dtype=jnp.int32) // EDGE_DEV
    slot_keys = edge_nodes.astype(jnp.int32) + (device_of * SLOT_ROWS)[None, :]
    endpoints = slot_table.reshape(-1)[slot_keys]
    live_mask = (jnp.arange(EDGES, dtype=jnp.int32) % EDGE_DEV < edge_count[device_of]).astype(jnp.float32)[:, None]
    graph = (slot_table, slot_keys, endpoints, live_mask)
    edge_list, node_list, edge_grads, node_grads, weight_lists = ([], [], [], [], [])
    for phase_index in range(N_PHASE):
        layer = (edge_w1[phase_index], edge_w2[phase_index], edge_vectors[phase_index], node_w1[phase_index], node_w2[phase_index], node_vectors[phase_index])
        edges_new, nodes_new, unused_edge, unused_node = forward(edges_fwd[phase_index], nodes_fwd[phase_index], layer, graph)
        edge_list.append(edges_new)
        node_list.append(nodes_new)
        edges_grad, nodes_grad, weight_grads = backward(edges_stash[phase_index], nodes_stash[phase_index], edge_cot[phase_index], node_cot[phase_index], layer, graph)
        edge_grads.append(edges_grad)
        node_grads.append(nodes_grad)
        weight_lists.append(weight_grads)
    next_edges = jnp.roll(jnp.stack(edge_list), 1, axis=0)
    next_nodes = jnp.roll(jnp.stack(node_list), 1, axis=0)
    prev_edge_grads = jnp.roll(jnp.stack(edge_grads), -1, axis=0)
    prev_node_grads = jnp.roll(jnp.stack(node_grads), -1, axis=0)
    stacked_grads = [jnp.stack([weights[index] for weights in weight_lists]) for index in range(6)]
    return (next_edges, next_nodes, prev_edge_grads, prev_node_grads, stacked_grads[0], stacked_grads[1], stacked_grads[2], stacked_grads[3], stacked_grads[4], stacked_grads[5])
```

```python
import jax
import jax.numpy as jnp
from jax import lax
from jax.experimental import pallas as pl
from jax.experimental.pallas import tpu as pltpu
from jax.sharding import PartitionSpec as P

TILE = 128
EPSILON = 1e-05
Z_SIZE = 8
GROUP = 8
F32 = jnp.float32
BF16 = jnp.bfloat16
MESH = pl.DeviceIdType.MESH
CHUNK = 256


def dot(a, b, contract=((1,), (0,))):
    return lax.dot_general(a, b, (contract, ((), ())), preferred_element_type=F32)


def dot_nt(a, b):
    return dot(a, b, ((1,), (1,)))


def dot_tn(a, b):
    return dot(a, b, ((0,), (0,)))


def layer_norm(pre_norm):
    row_mean = jnp.mean(pre_norm, axis=-1, keepdims=True)
    centered = pre_norm - row_mean
    row_var = jnp.mean(centered * centered, axis=-1, keepdims=True)
    inverse = lax.rsqrt(row_var + EPSILON)
    return centered * inverse, inverse


def norm_back(scaled, normed, inverse):
    mean_first = jnp.mean(scaled, axis=-1, keepdims=True)
    mean_second = jnp.mean(scaled * normed, axis=-1, keepdims=True)
    return inverse * (scaled - mean_first - normed * mean_second)


def to_slabs(rows):
    count = rows.shape[0] // 8
    left = rows[:, :128].reshape(count, 8, 128)
    right = rows[:, 128:].reshape(count, 8, 128)
    return jnp.concatenate([left, right], axis=1).astype(BF16)


def from_slabs(slabs):
    wide = slabs.astype(F32)
    count = wide.shape[0]
    left = wide[:, :8, :].reshape(count * 8, 128)
    right = wide[:, 8:, :].reshape(count * 8, 128)
    return jnp.concatenate([left, right], axis=1).astype(BF16)


def col_sum(rows):
    return jnp.sum(rows, axis=0, keepdims=True)


def rows_at(i, size=CHUNK):
    return pl.ds(pl.multiple_of(i * size, size), size)


def tick_kernel(
    dom_count,
    phase_count,
    ef, nf, es, ns, ec, nc, w1, w2, ev, nw1, nw2, nv, idx, sidx, cnt,
    o_ne, o_nn, o_pe, o_pn, o_ge, o_gn, o_gv,
    send_hot, send_hot_t, recv_hot, recv_hot_t, want_hot, want_hot_t,
    table_s, table_f, table_g, out_slab, in_slab,
    sent_rows, recv_rows, edge_pre, edge_hid, edge_norm, edge_inv, edge_pre_grad, edge_first_grad,
    node_pre, node_hid, node_norm, node_inv, agg_rows, node_first_grad, node_pre_grad,
    block_sums, own_s, own_f, base,
    new_edges, new_nodes, old_edges, old_nodes,
    g_edge, g_node, ra_edge, ra_node, sb, rb, fb, ab, va, vb, vec,
    x_send, x_recv, sh_send, sh_recv, ra_s, ra_r, rb_s, rb_r, gb_s, gb_r, ga_s, ga_r, v_s, v_r, local_sem,
):
    me = lax.axis_index("dom")
    phase = lax.axis_index("phase")
    zpos = lax.rem(me // 2, Z_SIZE)
    apos = (me // (2 * Z_SIZE)) * 2 + lax.rem(me, 2)
    features = ef.shape[1]
    node_dev = nf.shape[0]
    edge_dev = ef.shape[0]
    blocks = edge_dev // TILE
    own_tiles = node_dev // TILE
    mirror_tiles = (dom_count * 8) // TILE
    node_chunks = node_dev // CHUNK
    edge_chunks = edge_dev // CHUNK
    per_chunk = CHUNK // TILE

    def a_partner(k):
        other = lax.rem(apos + k, GROUP)
        return other, (other // 2) * (2 * Z_SIZE) + zpos * 2 + lax.rem(other, 2)

    def b_partner(k):
        other = lax.rem(zpos + k, Z_SIZE)
        return other, me + 2 * (other - zpos)

    barrier = pltpu.get_barrier_semaphore()

    def greet(k, carry):
        pl.semaphore_signal(
            barrier, inc=1, device_id={"dom": lax.rem(me + k, dom_count)}, device_id_type=MESH
        )
        return carry

    lax.fori_loop(1, dom_count, greet, 0)
    for step in (1, phase_count - 1):
        pl.semaphore_signal(
            barrier, inc=1, device_id={"phase": lax.rem(phase + step, phase_count)}, device_id_type=MESH
        )

    def start_exchange(x):
        def one(k, carry):
            other = lax.rem(me + k, dom_count)
            pltpu.make_async_remote_copy(
                out_slab.at[x, other], in_slab.at[x, me], x_send.at[x], x_recv.at[x],
                device_id={"dom": other}, device_id_type=MESH,
            ).start()
            return carry

        lax.fori_loop(1, dom_count, one, 0)
        in_slab[x, me] = out_slab[x, me]

    def exchange_all(x):
        part = pl.ds(0, dom_count - 1)
        return pltpu.make_async_remote_copy(
            out_slab.at[x, part], in_slab.at[x, part], x_send.at[x], x_recv.at[x],
            device_id={"dom": lax.rem(me + 1, dom_count)}, device_id_type=MESH,
        )

    def wait_exchange(x):
        exchange_all(x).wait_recv()
        return from_slabs(in_slab[x])

    def shift(slot, src, dst, step):
        return pltpu.make_async_remote_copy(
            src, dst, sh_send.at[slot], sh_recv.at[slot],
            device_id={"phase": lax.rem(phase + step, phase_count)}, device_id_type=MESH,
        )

    sub_iota = lax.broadcasted_iota(jnp.int32, (TILE, TILE), 0)
    lane_iota = lax.broadcasted_iota(jnp.int32, (TILE, TILE), 1)

    def build_want(b, carry):
        row = jnp.broadcast_to(idx[pl.ds(2 * blocks + b, 1), :], (TILE, TILE))
        col = jnp.transpose(row)
        for j in range(own_tiles):
            want_hot[rows_at(b, TILE), j * TILE:(j + 1) * TILE] = (col == lane_iota + j * TILE).astype(F32).astype(BF16)
        return carry

    lax.fori_loop(0, mirror_tiles, build_want, 0)

    def pick_rows(x, rows):
        def one(q, carry):
            picked = dot(want_hot[rows_at(q, TILE), :], rows[0:own_tiles].reshape(node_dev, features) if len(rows.shape) == 3 else rows[...])
            out_slab[x, pl.ds(pl.multiple_of(q * 16, 16), 16)] = to_slabs(picked)
            return carry

        lax.fori_loop(0, mirror_tiles, one, 0)

    pick_rows(0, ns)
    pl.semaphore_wait(barrier, dom_count - 1 + 2)
    start_exchange(0)
    pick_rows(1, nf)
    start_exchange(1)

    def build_edges(b, carry):
        for base_row, hot, hot_t in ((0, send_hot, send_hot_t), (blocks, recv_hot, recv_hot_t)):
            row = jnp.broadcast_to(jnp.bitwise_and(idx[pl.ds(base_row + b, 1), :], TILE - 1), (TILE, TILE))
            hot_t[b] = (row == sub_iota).astype(F32).astype(BF16)
            hot[b] = (jnp.transpose(row) == lane_iota).astype(F32).astype(BF16)
        return carry

    lax.fori_loop(0, blocks, build_edges, 0)

    for j in range(mirror_tiles):
        row = jnp.broadcast_to(idx[2 * blocks + j:2 * blocks + j + 1, :], (TILE, TILE))
        for i in range(own_tiles):
            want_hot_t[i * TILE:(i + 1) * TILE, j * TILE:(j + 1) * TILE] = (row == sub_iota + i * TILE).astype(F32).astype(BF16)

    table_s[0:own_tiles] = ns[...].reshape(own_tiles, TILE, features)
    table_f[0:own_tiles] = nf[...].reshape(own_tiles, TILE, features)

    def fetch(hot, b, table, first):
        return dot(hot[b], table[lax.div(sidx[first + b, 0], TILE)])

    def live_rows(i):
        at = lax.broadcasted_iota(jnp.int32, (CHUNK, features), 0) + i * CHUNK
        return jnp.where(at < cnt[0], 1.0, 0.0).astype(F32)

    def block_sum(hot_t, b, rows):
        high = rows.astype(BF16)
        low = (rows - high.astype(F32)).astype(BF16)
        return dot(jnp.concatenate([hot_t, hot_t], axis=1), jnp.concatenate([high, low], axis=0))

    def tile_total(k, first, count):
        total = jnp.zeros((TILE, features), F32)
        for b in range(count):
            tile = lax.div(idx[first + b:first + b + 1, 0:1], TILE)
            chosen = (tile == k).astype(F32)
            total = total + jnp.broadcast_to(chosen, (TILE, features)) * block_sums[b]
        return total

    def send_mirror_sums(x, first, count):
        def one(q, carry):
            total = tile_total(own_tiles + q, first, count)
            out_slab[x, pl.ds(pl.multiple_of(q * 16, 16), 16)] = to_slabs(total)
            return carry

        lax.fori_loop(0, mirror_tiles, one, 0)
        start_exchange(x)

    def own_sums(own, first, count):
        def one(k, carry):
            own[rows_at(k, TILE), :] = tile_total(k, first, count)
            return carry

        lax.fori_loop(0, own_tiles, one, 0)

    def edge_forward(edges, table, keep):
        def one(i, carry):
            rows = rows_at(i)
            from_send = jnp.concatenate(
                [fetch(send_hot, i * per_chunk + j, table, 0) for j in range(per_chunk)], axis=0
            ).astype(BF16)
            from_recv = jnp.concatenate(
                [fetch(recv_hot, i * per_chunk + j, table, blocks) for j in range(per_chunk)], axis=0
            ).astype(BF16)
            stacked = jnp.concatenate([edges[rows, :], from_send, from_recv], axis=1)
            pre = dot(stacked, w1[...]) + ev[0:1, :]
            hidden = jnp.maximum(pre, 0.0).astype(BF16)
            normed, inverse = layer_norm(dot(hidden, w2[...]) + ev[1:2, :])
            message = live_rows(i) * (normed * ev[2:3, :] + ev[3:4, :])
            if keep:
                sent_rows[rows, :] = from_send
                recv_rows[rows, :] = from_recv
                edge_pre[rows, :] = pre
                edge_hid[rows, :] = hidden
                edge_norm[rows, :] = normed
                edge_inv[rows, :] = inverse
            else:
                new_edges[rows, :] = (edges[rows, :].astype(F32) + message).astype(BF16)
            for j in range(per_chunk):
                b = i * per_chunk + j
                block_sums[b] = block_sum(recv_hot_t[b], b, message[j * TILE:(j + 1) * TILE, :])
            return carry

        lax.fori_loop(0, edge_chunks, one, 0)

    def node_forward(nodes, own, returned, keep):
        def one(i, carry):
            rows = rows_at(i)
            total = own[rows, :] + dot(want_hot_t[rows, :], returned)
            gathered = total.astype(BF16)
            stacked = jnp.concatenate([nodes[rows, :], gathered], axis=1)
            pre = dot(stacked, nw1[...]) + nv[0:1, :]
            hidden = jnp.maximum(pre, 0.0).astype(BF16)
            normed, inverse = layer_norm(dot(hidden, nw2[...]) + nv[1:2, :])
            if keep:
                agg_rows[rows, :] = gathered
                node_pre[rows, :] = pre
                node_hid[rows, :] = hidden
                node_norm[rows, :] = normed
                node_inv[rows, :] = inverse
            else:
                new_nodes[rows, :] = (
                    nodes[rows, :].astype(F32) + (normed * nv[2:3, :] + nv[3:4, :])
                ).astype(BF16)
            return carry

        lax.fori_loop(0, node_chunks, one, 0)

    table_s[own_tiles:] = wait_exchange(0).reshape(mirror_tiles, TILE, features)
    edge_forward(es, table_s, True)
    send_mirror_sums(2, blocks, blocks)
    own_sums(own_s, blocks, blocks)

    table_f[own_tiles:] = wait_exchange(1).reshape(mirror_tiles, TILE, features)
    edge_forward(ef, table_f, False)
    send_mirror_sums(3, blocks, blocks)
    shift(0, new_edges, o_ne, 1).start()
    own_sums(own_f, blocks, blocks)

    node_forward(ns, own_s, wait_exchange(2), True)

    def node_back(i, carry):
        s_first, s_pre, s_gain, s_shift = carry
        rows = rows_at(i)
        top = nc[rows, :].astype(F32)
        normed = node_norm[rows, :]
        pre_grad = norm_back(top * nv[2:3, :], normed, node_inv[rows, :]).astype(BF16)
        first = jnp.where(node_pre[rows, :] > 0.0, dot_nt(pre_grad, nw2[...]), 0.0).astype(BF16)
        node_pre_grad[rows, :] = pre_grad
        node_first_grad[rows, :] = first
        table_g[rows_at(i, per_chunk)] = dot_nt(first, nw1[features:, :]).astype(BF16).reshape(per_chunk, TILE, features)
        return (
            s_first + col_sum(first.astype(F32)),
            s_pre + col_sum(pre_grad.astype(F32)),
            s_gain + col_sum(top * normed),
            s_shift + col_sum(top),
        )

    zero_row = jnp.zeros((1, features), F32)
    sums = lax.fori_loop(0, node_chunks, node_back, (zero_row,) * 4)
    for j in range(4):
        vec[4 + j:5 + j, :] = sums[j]

    pick_rows(4, table_g)
    start_exchange(4)

    def start_a(which, grads, arrived, used):
        arrived[apos] = grads[apos]
        for k in range(1, GROUP):
            other, device = a_partner(k)
            pltpu.make_async_remote_copy(
                grads.at[other, pl.ds(0, used)], arrived.at[apos, pl.ds(0, used)],
                ra_s.at[which], ra_r.at[which], device_id={"dom": device}, device_id_type=MESH,
            ).start()

    def all_a(which, grads, arrived, used):
        part = pl.ds(0, GROUP - 1)
        return pltpu.make_async_remote_copy(
            grads.at[part, pl.ds(0, used)], arrived.at[part, pl.ds(0, used)],
            ra_s.at[which], ra_r.at[which], device_id={"dom": a_partner(1)[1]}, device_id_type=MESH,
        )

    def start_b(which, arrived):
        total = arrived[0].astype(F32)
        for k in range(1, GROUP):
            total = total + arrived[k].astype(F32)
        sb[which] = total.astype(BF16).reshape(Z_SIZE, 16, features)
        rb[which, zpos] = sb[which, zpos]
        for k in range(1, Z_SIZE):
            other, device = b_partner(k)
            pltpu.make_async_remote_copy(
                sb.at[which, other], rb.at[which, zpos], rb_s.at[which], rb_r.at[which],
                device_id={"dom": device}, device_id_type=MESH,
            ).start()

    def all_b(which):
        part = pl.ds(0, Z_SIZE - 1)
        return pltpu.make_async_remote_copy(
            sb.at[which, part], rb.at[which, part], rb_s.at[which], rb_r.at[which],
            device_id={"dom": b_partner(1)[1]}, device_id_type=MESH,
        )

    def start_gather_b(which):
        total = rb[which, 0].astype(F32)
        for k in range(1, Z_SIZE):
            total = total + rb[which, k].astype(F32)
        fb[which] = total.astype(BF16)
        ab[which, zpos] = fb[which]
        for k in range(1, Z_SIZE):
            other, device = b_partner(k)
            pltpu.make_async_remote_copy(
                fb.at[which], ab.at[which, zpos], gb_s.at[which], gb_r.at[which],
                device_id={"dom": device}, device_id_type=MESH,
            ).start()

    def all_gather_b(which):
        part = pl.ds(0, Z_SIZE - 1)
        return pltpu.make_async_remote_copy(
            ab.at[which, part], ab.at[which, part], gb_s.at[which], gb_r.at[which],
            device_id={"dom": b_partner(1)[1]}, device_id_type=MESH,
        )

    def start_gather_a(which, out):
        pltpu.make_async_copy(ab.at[which], out.at[apos], local_sem.at[which]).start()
        for k in range(1, GROUP):
            other, device = a_partner(k)
            pltpu.make_async_remote_copy(
                ab.at[which], out.at[apos], ga_s.at[which], ga_r.at[which],
                device_id={"dom": device}, device_id_type=MESH,
            ).start()

    def all_gather_a(which, out):
        part = pl.ds(0, GROUP - 1)
        return pltpu.make_async_remote_copy(
            out.at[part], out.at[part], ga_s.at[which], ga_r.at[which],
            device_id={"dom": a_partner(1)[1]}, device_id_type=MESH,
        )

    node_used = (3 * features) // GROUP

    def put_node_grads(first_row, grad):
        at = 0
        while at < grad.shape[0]:
            share, inner = divmod(first_row + at, node_used)
            size = min(node_used - inner, grad.shape[0] - at)
            g_node[share, inner:inner + size, :] = grad[at:at + size, :].astype(BF16)
            at += size

    for j in range(GROUP):
        g_node[j, node_used:, :] = jnp.zeros((TILE - node_used, features), BF16)
        ra_node[j, node_used:, :] = jnp.zeros((TILE - node_used, features), BF16)
    put_node_grads(0, dot_tn(ns[...], node_first_grad[...]))
    put_node_grads(features, dot_tn(agg_rows[...], node_first_grad[...]))
    put_node_grads(2 * features, dot_tn(node_hid[...], node_pre_grad[...]))
    start_a(0, g_node, ra_node, node_used)

    def node_base(i, carry):
        rows = rows_at(i)
        base[rows, :] = nc[rows, :].astype(F32) + dot_nt(node_first_grad[rows, :], nw1[:features, :])
        return carry

    lax.fori_loop(0, node_chunks, node_base, 0)

    node_forward(nf, own_f, wait_exchange(3), False)
    shift(1, new_nodes, o_nn, 1).start()

    all_a(0, g_node, ra_node, node_used).wait_recv()
    start_b(0, ra_node)

    table_g[own_tiles:] = wait_exchange(4).reshape(mirror_tiles, TILE, features)

    def edge_back(i, carry):
        s_first, s_pre, s_gain, s_shift = carry
        rows = rows_at(i)
        from_recv = jnp.concatenate(
            [fetch(recv_hot, i * per_chunk + j, table_g, blocks) for j in range(per_chunk)], axis=0
        )
        top = live_rows(i) * (ec[rows, :].astype(F32) + from_recv)
        normed = edge_norm[rows, :]
        pre_grad = norm_back(top * ev[2:3, :], normed, edge_inv[rows, :]).astype(BF16)
        first = jnp.where(edge_pre[rows, :] > 0.0, dot_nt(pre_grad, w2[...]), 0.0).astype(BF16)
        edge_pre_grad[rows, :] = pre_grad
        edge_first_grad[rows, :] = first
        to_send = dot_nt(first, w1[features:2 * features, :])
        to_recv = dot_nt(first, w1[2 * features:, :])
        for j in range(per_chunk):
            b = i * per_chunk + j
            block_sums[b] = block_sum(send_hot_t[b], b, to_send[j * TILE:(j + 1) * TILE, :])
            block_sums[blocks + b] = block_sum(recv_hot_t[b], b, to_recv[j * TILE:(j + 1) * TILE, :])
        return (
            s_first + col_sum(first.astype(F32)),
            s_pre + col_sum(pre_grad.astype(F32)),
            s_gain + col_sum(top * normed),
            s_shift + col_sum(top),
        )

    sums = lax.fori_loop(0, edge_chunks, edge_back, (zero_row,) * 4)
    for j in range(4):
        vec[j:j + 1, :] = sums[j]
    send_mirror_sums(5, 0, 2 * blocks)

    va[apos] = vec[...]
    for k in range(1, GROUP):
        other, device = a_partner(k)
        pltpu.make_async_remote_copy(
            vec, va.at[apos], v_s.at[0], v_r.at[0], device_id={"dom": device}, device_id_type=MESH
        ).start()

    def edge_out(i, carry):
        rows = rows_at(i)
        old_edges[rows, :] = (
            ec[rows, :].astype(F32) + dot_nt(edge_first_grad[rows, :], w1[:features, :])
        ).astype(BF16)
        return carry

    lax.fori_loop(0, edge_chunks, edge_out, 0)
    shift(2, old_edges, o_pe, phase_count - 1).start()

    for part, rows in enumerate((es, sent_rows, recv_rows)):
        grad = dot_tn(rows[...], edge_first_grad[...]).astype(BF16)
        g_edge[2 * part] = grad[:TILE, :]
        g_edge[2 * part + 1] = grad[TILE:, :]
    grad = dot_tn(edge_hid[...], edge_pre_grad[...]).astype(BF16)
    g_edge[6] = grad[:TILE, :]
    g_edge[7] = grad[TILE:, :]
    start_a(1, g_edge, ra_edge, TILE)

    own_sums(own_s, 0, 2 * blocks)
    all_b(0).wait_recv()
    start_gather_b(0)

    returned = wait_exchange(5)

    def node_out(i, carry):
        rows = rows_at(i)
        old_nodes[rows, :] = (
            base[rows, :] + own_s[rows, :] + dot(want_hot_t[rows, :], returned)
        ).astype(BF16)
        shift(3, old_nodes.at[rows, :], o_pn.at[rows, :], phase_count - 1).start()
        return carry

    lax.fori_loop(0, node_chunks, node_out, 0)

    all_a(1, g_edge, ra_edge, TILE).wait_recv()
    start_b(1, ra_edge)
    all_gather_b(0).wait_recv()
    start_gather_a(0, o_gn)

    group_part = pl.ds(0, GROUP - 1)
    first_all = pltpu.make_async_remote_copy(
        va.at[group_part], va.at[group_part], v_s.at[0], v_r.at[0],
        device_id={"dom": a_partner(1)[1]}, device_id_type=MESH,
    )
    first_all.wait_recv()
    first_all.wait_send()
    total = va[0]
    for k in range(1, GROUP):
        total = total + va[k]
    vec[...] = total
    vb[zpos] = total
    for k in range(1, Z_SIZE):
        other, device = b_partner(k)
        pltpu.make_async_remote_copy(
            vec, vb.at[zpos], v_s.at[1], v_r.at[1], device_id={"dom": device}, device_id_type=MESH
        ).start()

    all_b(1).wait_recv()
    start_gather_b(1)
    second_all = pltpu.make_async_remote_copy(
        vb.at[group_part], vb.at[group_part], v_s.at[1], v_r.at[1],
        device_id={"dom": b_partner(1)[1]}, device_id_type=MESH,
    )
    second_all.wait_recv()
    total = vb[0]
    for k in range(1, Z_SIZE):
        total = total + vb[k]
    o_gv[...] = total
    all_gather_b(1).wait_recv()
    start_gather_a(1, o_ge)

    for x in range(6):
        exchange_all(x).wait_send()
    all_a(0, g_node, ra_node, node_used).wait_send()
    all_a(1, g_edge, ra_edge, TILE).wait_send()
    second_all.wait_send()
    for which, out in ((0, o_gn), (1, o_ge)):
        all_b(which).wait_send()
        all_gather_b(which).wait_send()
        pltpu.make_async_copy(ab.at[which], out.at[apos], local_sem.at[which]).wait()
        all_gather_a(which, out).wait_send()
        all_gather_a(which, out).wait_recv()
    shift(0, new_edges, o_ne, 1).wait()
    shift(1, new_nodes, o_nn, 1).wait()
    shift(2, old_edges, o_pe, phase_count - 1).wait()
    shift(3, old_nodes, o_pn, phase_count - 1).wait()


def tick(dom_count, phase_count, *arrays):
    edge_dev, features = arrays[0].shape
    node_dev = arrays[1].shape[0]
    blocks = edge_dev // TILE
    slots = node_dev + dom_count * 8
    vmem = lambda shape, kind=BF16: pltpu.VMEM(shape, kind)
    sem = lambda count: pltpu.SemaphoreType.DMA((count,))
    scratch = (
        [vmem((blocks, TILE, TILE))] * 4
        + [vmem((dom_count * 8, node_dev)), vmem((node_dev, dom_count * 8))]
        + [vmem((slots // TILE, TILE, features))] * 3
        + [vmem((6, dom_count, 16, 128))] * 2
        + [vmem((edge_dev, features))] * 2
        + [vmem((edge_dev, features), F32), vmem((edge_dev, features)), vmem((edge_dev, features), F32), vmem((edge_dev, 1), F32)]
        + [vmem((edge_dev, features))] * 2
        + [vmem((node_dev, features), F32), vmem((node_dev, features)), vmem((node_dev, features), F32), vmem((node_dev, 1), F32)]
        + [vmem((node_dev, features))] * 3
        + [vmem((2 * blocks, TILE, features), F32)]
        + [vmem((node_dev, features), F32)] * 3
        + [vmem((edge_dev, features)), vmem((node_dev, features))] * 2
        + [vmem((GROUP, TILE, features))] * 4
        + [vmem((2, Z_SIZE, 16, features))] * 2
        + [vmem((2, 16, features)), vmem((2, Z_SIZE, 16, features))]
        + [vmem((GROUP, 8, features), F32), vmem((Z_SIZE, 8, features), F32), vmem((8, features), F32)]
        + [sem(6), sem(6), sem(4), sem(4)]
        + [sem(2)] * 11
    )
    in_vmem = pl.BlockSpec(memory_space=pltpu.VMEM)
    in_smem = pl.BlockSpec(memory_space=pltpu.SMEM)
    anywhere = pl.BlockSpec(memory_space=pl.ANY)
    out_shape = (
        jax.ShapeDtypeStruct((edge_dev, features), BF16),
        jax.ShapeDtypeStruct((node_dev, features), BF16),
        jax.ShapeDtypeStruct((edge_dev, features), BF16),
        jax.ShapeDtypeStruct((node_dev, features), BF16),
        jax.ShapeDtypeStruct((GROUP, Z_SIZE, 16, features), BF16),
        jax.ShapeDtypeStruct((GROUP, Z_SIZE, 16, features), BF16),
        jax.ShapeDtypeStruct((8, features), F32),
    )

    def kernel(*refs):
        tick_kernel(dom_count, phase_count, *refs)

    return pl.pallas_call(
        kernel,
        out_shape=out_shape,
        in_specs=[in_vmem] * 13 + [in_smem] * 2,
        out_specs=[anywhere] * 6 + [in_vmem],
        scratch_shapes=scratch,
        name="tick",
        compiler_params=pltpu.CompilerParams(
            collective_id=0, has_side_effects=True, vmem_limit_bytes=48 * 2**20
        ),
    )(*arrays)


def on_device(
    edges_fwd, nodes_fwd, edges_stash, nodes_stash, edge_cot, node_cot,
    edge_w1, edge_w2, edge_vectors, node_w1, node_w2, node_vectors,
    edge_nodes, mirror_rows, edge_count,
):
    dom_count = lax.axis_size("dom")
    phase_count = lax.axis_size("phase")
    features = edges_fwd.shape[2]
    rows = jnp.concatenate(
        [edge_nodes.reshape(-1, TILE), mirror_rows.reshape(-1, TILE)], axis=0
    ).astype(jnp.int32)
    ne, nn, pe, pn, ge, gn, gv = tick(
        dom_count, phase_count,
        edges_fwd[0], nodes_fwd[0], edges_stash[0], nodes_stash[0], edge_cot[0], node_cot[0],
        edge_w1[0], edge_w2[0], edge_vectors[0], node_w1[0], node_w2[0], node_vectors[0],
        rows, rows, edge_count,
    )
    ge = ge.reshape(-1, features)
    node_used = (3 * features) // GROUP
    gn = gn.reshape(GROUP, TILE, features)[:, :node_used].reshape(-1, features)
    return (
        ne[None], nn[None], pe[None], pn[None],
        ge[: 3 * features].astype(F32)[None],
        ge[3 * features :].astype(F32)[None],
        gv[:4][None],
        gn[: 2 * features].astype(F32)[None],
        gn[2 * features :].astype(F32)[None],
        gv[4:][None],
    )


def solution(mesh):
    rows = P("phase", "dom", None)
    whole = P("phase", None, None)
    in_specs = (rows,) * 6 + (whole,) * 6 + (P(None, "dom"), P("dom", None, None), P("dom"))
    out_specs = (rows,) * 4 + (whole,) * 6
    return jax.shard_map(
        on_device, mesh=mesh, in_specs=in_specs, out_specs=out_specs, check_vma=False
    )
```

```python
import jax
import jax.numpy as jnp
from jax import lax
from jax.experimental import pallas as pl
from jax.experimental.pallas import tpu as pltpu
from jax.sharding import PartitionSpec as P

TILE = 128
EPSILON = 1e-05
Z_SIZE = 8
GROUP = 8
F32 = jnp.float32
BF16 = jnp.bfloat16
MESH = pl.DeviceIdType.MESH
EDGE_CHUNK = 768
NODE_CHUNK = 1024
UNROLL = False
VMEM_BYTES = 63 * 2**20


def dot(a, b, contract=((1,), (0,))):
    return lax.dot_general(a, b, (contract, ((), ())), preferred_element_type=F32)


def dot_nt(a, b):
    return dot(a, b, ((1,), (1,)))


def dot_tn(a, b):
    return dot(a, b, ((0,), (0,)))


def layer_norm(pre_norm):
    row_mean = jnp.mean(pre_norm, axis=-1, keepdims=True)
    centered = pre_norm - row_mean
    row_var = jnp.mean(centered * centered, axis=-1, keepdims=True)
    inverse = lax.rsqrt(row_var + EPSILON)
    return centered * inverse, inverse


def norm_back(scaled, normed, inverse):
    mean_first = jnp.mean(scaled, axis=-1, keepdims=True)
    mean_second = jnp.mean(scaled * normed, axis=-1, keepdims=True)
    return inverse * (scaled - mean_first - normed * mean_second)


def to_slabs(rows):
    count = rows.shape[0] // 8
    left = rows[:, :128].reshape(count, 8, 128)
    right = rows[:, 128:].reshape(count, 8, 128)
    return jnp.concatenate([left, right], axis=1).astype(BF16)


def from_slabs(slabs):
    wide = slabs.astype(F32)
    count = wide.shape[0]
    left = wide[:, :8, :].reshape(count * 8, 128)
    right = wide[:, 8:, :].reshape(count * 8, 128)
    return jnp.concatenate([left, right], axis=1).astype(BF16)


def col_sum(rows):
    return jnp.sum(rows, axis=0, keepdims=True)


def rows_at(i, size):
    return pl.ds(pl.multiple_of(i * size, size), size)


def tick_kernel(
    dom_count,
    phase_count,
    h_ef, h_nf, h_es, h_ns, h_ec, h_nc, h_w1, h_w2, h_ev, h_nw1, h_nw2, h_nv, ends, mirror, s_ends, cnt,
    o_ne, o_nn, o_pe, o_pn, o_ge, o_gn, o_gv,
    ef, nf, es, ns, ec, nc, w1, w2, ev, nw1, nw2, nv, want_row,
    send_hot, send_hot_t, recv_hot, recv_hot_t, want_hot, want_hot_t,
    table_s, table_f, table_g, out_slab, in_slab,
    sent_rows, recv_rows, edge_pre, edge_hid, edge_norm, edge_inv, edge_pre_grad, edge_first_grad,
    node_pre, node_hid, node_norm, node_inv, agg_rows, node_first_grad, node_pre_grad,
    block_sums, own_s, own_f, base,
    new_edges, new_nodes, old_edges, old_nodes,
    g_edge, g_node, ra_edge, ra_node, sb, rb, fb, ab, va, vb, vec,
    x_send, x_recv, sh_send, sh_recv, ra_s, ra_r, rb_s, rb_r, gb_s, gb_r, ga_s, ga_r, v_s, v_r, local_sem, in_sem,
):
    me = lax.axis_index("dom")
    phase = lax.axis_index("phase")
    zpos = lax.rem(me // 2, Z_SIZE)
    apos = (me // (2 * Z_SIZE)) * 2 + lax.rem(me, 2)
    features = ef.shape[1]
    node_dev = nf.shape[0]
    edge_dev = ef.shape[0]
    blocks = edge_dev // TILE
    own_tiles = node_dev // TILE
    mirror_tiles = (dom_count * 8) // TILE
    node_chunks = node_dev // NODE_CHUNK
    edge_chunks = edge_dev // EDGE_CHUNK
    per_chunk = EDGE_CHUNK // TILE

    def a_partner(k):
        other = lax.rem(apos + k, GROUP)
        return other, (other // 2) * (2 * Z_SIZE) + zpos * 2 + lax.rem(other, 2)

    def b_partner(k):
        other = lax.rem(zpos + k, Z_SIZE)
        return other, me + 2 * (other - zpos)

    operands = [
        (h_ns, ns), (h_nf, nf), (h_es, es), (h_w1, w1), (h_w2, w2), (h_ev, ev), (h_ef, ef),
        (h_nw1, nw1), (h_nw2, nw2), (h_nv, nv), (h_nc, nc), (h_ec, ec),
    ]

    def operand(n):
        return pltpu.make_async_copy(operands[n][0], operands[n][1], in_sem.at[n])

    for n in range(len(operands)):
        operand(n).start()

    barrier = pltpu.get_barrier_semaphore()

    def greet(k, carry):
        pl.semaphore_signal(
            barrier, inc=1, device_id={"dom": lax.rem(me + k, dom_count)}, device_id_type=MESH
        )
        return carry

    lax.fori_loop(1, dom_count, greet, 0)
    for step in (1, phase_count - 1):
        pl.semaphore_signal(
            barrier, inc=1, device_id={"phase": lax.rem(phase + step, phase_count)}, device_id_type=MESH
        )

    def start_exchange(x):
        def one(k, carry):
            other = lax.rem(me + k, dom_count)
            pltpu.make_async_remote_copy(
                out_slab.at[x, other], in_slab.at[x, me], x_send.at[x], x_recv.at[x],
                device_id={"dom": other}, device_id_type=MESH,
            ).start()
            return carry

        lax.fori_loop(1, dom_count, one, 0)
        in_slab[x, me] = out_slab[x, me]

    def exchange_all(x):
        part = pl.ds(0, dom_count - 1)
        return pltpu.make_async_remote_copy(
            out_slab.at[x, part], in_slab.at[x, part], x_send.at[x], x_recv.at[x],
            device_id={"dom": lax.rem(me + 1, dom_count)}, device_id_type=MESH,
        )

    def wait_exchange(x):
        exchange_all(x).wait_recv()
        return from_slabs(in_slab[x])

    def shift(slot, src, dst, step):
        return pltpu.make_async_remote_copy(
            src, dst, sh_send.at[slot], sh_recv.at[slot],
            device_id={"phase": lax.rem(phase + step, phase_count)}, device_id_type=MESH,
        )

    sub_iota = lax.broadcasted_iota(jnp.int32, (TILE, TILE), 0)
    lane_iota = lax.broadcasted_iota(jnp.int32, (TILE, TILE), 1)

    slab_iota = lax.broadcasted_iota(jnp.int32, (TILE, dom_count), 0)
    dom_iota = lax.broadcasted_iota(jnp.int32, (TILE, dom_count), 1)
    in_slab_iota = lax.broadcasted_iota(jnp.int32, (TILE, 8), 0)
    cap_iota = lax.broadcasted_iota(jnp.int32, (TILE, 8), 1)
    lane_float = lane_iota.astype(F32)
    sub_float = sub_iota.astype(F32)
    mirror_high = lax.div(mirror[...], 8).astype(F32).astype(BF16)
    mirror_low = lax.rem(mirror[...], 8).astype(F32).astype(BF16)

    def build_want(b, carry):
        owner = (dom_iota == b * 16 + lax.div(slab_iota, 8)).astype(F32).astype(BF16)
        named = dot_nt(owner, mirror_high) * 8.0 + dot_nt(owner, mirror_low)
        named = jnp.where(cap_iota == lax.rem(in_slab_iota, 8), named, 0.0)
        col = jnp.broadcast_to(jnp.sum(named, axis=1, keepdims=True), (TILE, TILE))
        want_row[b] = jnp.transpose(col)[:8]
        for j in range(own_tiles):
            want_hot[rows_at(b, TILE), j * TILE:(j + 1) * TILE] = (col == lane_float + float(j * TILE)).astype(F32).astype(BF16)
        return carry

    lax.fori_loop(0, mirror_tiles, build_want, 0)

    def pick_rows(x, rows):
        def one(q, carry):
            picked = dot(want_hot[rows_at(q, TILE), :], rows[0:own_tiles].reshape(node_dev, features) if len(rows.shape) == 3 else rows[...])
            out_slab[x, pl.ds(pl.multiple_of(q * 16, 16), 16)] = to_slabs(picked)
            return carry

        lax.fori_loop(0, mirror_tiles, one, 0)

    operand(0).wait()
    pick_rows(0, ns)
    pl.semaphore_wait(barrier, dom_count - 1 + 2)
    start_exchange(0)
    operand(1).wait()
    pick_rows(1, nf)
    start_exchange(1)

    def build_edges(b, carry):
        for end, hot, hot_t in ((0, send_hot, send_hot_t), (1, recv_hot, recv_hot_t)):
            row = jnp.broadcast_to(jnp.bitwise_and(ends[end:end + 1, rows_at(b, TILE)], TILE - 1), (TILE, TILE))
            hot_t[b] = (row == sub_iota).astype(F32).astype(BF16)
            hot[b] = (jnp.transpose(row) == lane_iota).astype(F32).astype(BF16)
        return carry

    lax.fori_loop(0, blocks, build_edges, 0)

    for j in range(mirror_tiles):
        row = jnp.broadcast_to(want_row[j, 0:1, :], (TILE, TILE))
        for i in range(own_tiles):
            want_hot_t[i * TILE:(i + 1) * TILE, j * TILE:(j + 1) * TILE] = (row == sub_float + float(i * TILE)).astype(F32).astype(BF16)

    table_s[0:own_tiles] = ns[...].reshape(own_tiles, TILE, features)
    table_f[0:own_tiles] = nf[...].reshape(own_tiles, TILE, features)

    def fetch(hot, b, table, end):
        return dot(hot[b], table[lax.div(s_ends[end, b * TILE], TILE)])

    def live_rows(i):
        at = lax.broadcasted_iota(jnp.int32, (EDGE_CHUNK, features), 0) + i * EDGE_CHUNK
        return jnp.where(at < cnt[0], 1.0, 0.0).astype(F32)

    def block_sum(hot_t, b, rows):
        high = rows.astype(BF16)
        low = (rows - high.astype(F32)).astype(BF16)
        return dot(jnp.concatenate([hot_t, hot_t], axis=1), jnp.concatenate([high, low], axis=0))

    def tile_total(k, first, count):
        total = jnp.zeros((TILE, features), F32)
        for b in range(count):
            end, block = divmod(first + b, blocks)
            tile = lax.div(ends[end:end + 1, block * TILE:block * TILE + 1], TILE)
            chosen = (tile == k).astype(F32)
            total = total + jnp.broadcast_to(chosen, (TILE, features)) * block_sums[b]
        return total

    def send_mirror_sums(x, first, count):
        def one(q, carry):
            total = tile_total(own_tiles + q, first, count)
            out_slab[x, pl.ds(pl.multiple_of(q * 16, 16), 16)] = to_slabs(total)
            return carry

        lax.fori_loop(0, mirror_tiles, one, 0)
        start_exchange(x)

    def own_sums(own, first, count):
        def one(k, carry):
            own[rows_at(k, TILE), :] = tile_total(k, first, count)
            return carry

        lax.fori_loop(0, own_tiles, one, 0)

    def edge_forward(edges, table, keep):
        def one(i, carry):
            rows = rows_at(i, EDGE_CHUNK)
            from_send = jnp.concatenate(
                [fetch(send_hot, i * per_chunk + j, table, 0) for j in range(per_chunk)], axis=0
            ).astype(BF16)
            from_recv = jnp.concatenate(
                [fetch(recv_hot, i * per_chunk + j, table, 1) for j in range(per_chunk)], axis=0
            ).astype(BF16)
            stacked = jnp.concatenate([edges[rows, :], from_send, from_recv], axis=1)
            pre = dot(stacked, w1[...]) + ev[0:1, :]
            hidden = jnp.maximum(pre, 0.0).astype(BF16)
            normed, inverse = layer_norm(dot(hidden, w2[...]) + ev[1:2, :])
            message = live_rows(i) * (normed * ev[2:3, :] + ev[3:4, :])
            if keep:
                sent_rows[rows, :] = from_send
                recv_rows[rows, :] = from_recv
                edge_pre[rows, :] = pre
                edge_hid[rows, :] = hidden
                edge_norm[rows, :] = normed
                edge_inv[rows, :] = inverse
            else:
                new_edges[rows, :] = (edges[rows, :].astype(F32) + message).astype(BF16)
            for j in range(per_chunk):
                b = i * per_chunk + j
                block_sums[b] = block_sum(recv_hot_t[b], b, message[j * TILE:(j + 1) * TILE, :])
            return carry

        lax.fori_loop(0, edge_chunks, one, 0, unroll=UNROLL)

    def node_forward(nodes, own, returned, keep):
        def one(i, carry):
            rows = rows_at(i, NODE_CHUNK)
            total = own[rows, :] + dot(want_hot_t[rows, :], returned)
            gathered = total.astype(BF16)
            stacked = jnp.concatenate([nodes[rows, :], gathered], axis=1)
            pre = dot(stacked, nw1[...]) + nv[0:1, :]
            hidden = jnp.maximum(pre, 0.0).astype(BF16)
            normed, inverse = layer_norm(dot(hidden, nw2[...]) + nv[1:2, :])
            if keep:
                agg_rows[rows, :] = gathered
                node_pre[rows, :] = pre
                node_hid[rows, :] = hidden
                node_norm[rows, :] = normed
                node_inv[rows, :] = inverse
            else:
                new_nodes[rows, :] = (
                    nodes[rows, :].astype(F32) + (normed * nv[2:3, :] + nv[3:4, :])
                ).astype(BF16)
            return carry

        lax.fori_loop(0, node_chunks, one, 0, unroll=UNROLL)

    for n in (2, 3, 4, 5):
        operand(n).wait()
    table_s[own_tiles:] = wait_exchange(0).reshape(mirror_tiles, TILE, features)
    edge_forward(es, table_s, True)
    send_mirror_sums(2, blocks, blocks)
    own_sums(own_s, blocks, blocks)

    operand(6).wait()
    table_f[own_tiles:] = wait_exchange(1).reshape(mirror_tiles, TILE, features)
    edge_forward(ef, table_f, False)
    send_mirror_sums(3, blocks, blocks)
    shift(0, new_edges, o_ne, 1).start()
    own_sums(own_f, blocks, blocks)

    for n in (7, 8, 9, 10):
        operand(n).wait()
    node_forward(ns, own_s, wait_exchange(2), True)

    def node_back(i, carry):
        s_first, s_pre, s_gain, s_shift = carry
        rows = rows_at(i, NODE_CHUNK)
        top = nc[rows, :].astype(F32)
        normed = node_norm[rows, :]
        pre_grad = norm_back(top * nv[2:3, :], normed, node_inv[rows, :]).astype(BF16)
        first = jnp.where(node_pre[rows, :] > 0.0, dot_nt(pre_grad, nw2[...]), 0.0).astype(BF16)
        node_pre_grad[rows, :] = pre_grad
        node_first_grad[rows, :] = first
        table_g[rows_at(i, NODE_CHUNK // TILE)] = dot_nt(first, nw1[features:, :]).astype(BF16).reshape(NODE_CHUNK // TILE, TILE, features)
        return (
            s_first + col_sum(first.astype(F32)),
            s_pre + col_sum(pre_grad.astype(F32)),
            s_gain + col_sum(top * normed),
            s_shift + col_sum(top),
        )

    zero_row = jnp.zeros((1, features), F32)
    sums = lax.fori_loop(0, node_chunks, node_back, (zero_row,) * 4, unroll=UNROLL)
    for j in range(4):
        vec[4 + j:5 + j, :] = sums[j]

    pick_rows(4, table_g)
    start_exchange(4)

    def start_a(which, grads, arrived, used):
        arrived[apos] = grads[apos]
        for k in range(1, GROUP):
            other, device = a_partner(k)
            pltpu.make_async_remote_copy(
                grads.at[other, pl.ds(0, used)], arrived.at[apos, pl.ds(0, used)],
                ra_s.at[which], ra_r.at[which], device_id={"dom": device}, device_id_type=MESH,
            ).start()

    def all_a(which, grads, arrived, used):
        part = pl.ds(0, GROUP - 1)
        return pltpu.make_async_remote_copy(
            grads.at[part, pl.ds(0, used)], arrived.at[part, pl.ds(0, used)],
            ra_s.at[which], ra_r.at[which], device_id={"dom": a_partner(1)[1]}, device_id_type=MESH,
        )

    def start_b(which, arrived):
        total = arrived[0].astype(F32)
        for k in range(1, GROUP):
            total = total + arrived[k].astype(F32)
        sb[which] = total.astype(BF16).reshape(Z_SIZE, 16, features)
        rb[which, zpos] = sb[which, zpos]
        for k in range(1, Z_SIZE):
            other, device = b_partner(k)
            pltpu.make_async_remote_copy(
                sb.at[which, other], rb.at[which, zpos], rb_s.at[which], rb_r.at[which],
                device_id={"dom": device}, device_id_type=MESH,
            ).start()

    def all_b(which):
        part = pl.ds(0, Z_SIZE - 1)
        return pltpu.make_async_remote_copy(
            sb.at[which, part], rb.at[which, part], rb_s.at[which], rb_r.at[which],
            device_id={"dom": b_partner(1)[1]}, device_id_type=MESH,
        )

    def start_gather_b(which):
        total = rb[which, 0].astype(F32)
        for k in range(1, Z_SIZE):
            total = total + rb[which, k].astype(F32)
        fb[which] = total.astype(BF16)
        ab[which, zpos] = fb[which]
        for k in range(1, Z_SIZE):
            other, device = b_partner(k)
            pltpu.make_async_remote_copy(
                fb.at[which], ab.at[which, zpos], gb_s.at[which], gb_r.at[which],
                device_id={"dom": device}, device_id_type=MESH,
            ).start()

    def all_gather_b(which):
        part = pl.ds(0, Z_SIZE - 1)
        return pltpu.make_async_remote_copy(
            ab.at[which, part], ab.at[which, part], gb_s.at[which], gb_r.at[which],
            device_id={"dom": b_partner(1)[1]}, device_id_type=MESH,
        )

    def start_gather_a(which, out):
        pltpu.make_async_copy(ab.at[which], out.at[apos], local_sem.at[which]).start()
        for k in range(1, GROUP):
            other, device = a_partner(k)
            pltpu.make_async_remote_copy(
                ab.at[which], out.at[apos], ga_s.at[which], ga_r.at[which],
                device_id={"dom": device}, device_id_type=MESH,
            ).start()

    def all_gather_a(which, out):
        part = pl.ds(0, GROUP - 1)
        return pltpu.make_async_remote_copy(
            out.at[part], out.at[part], ga_s.at[which], ga_r.at[which],
            device_id={"dom": a_partner(1)[1]}, device_id_type=MESH,
        )

    node_used = (3 * features) // GROUP

    def put_node_grads(first_row, grad):
        at = 0
        while at < grad.shape[0]:
            share, inner = divmod(first_row + at, node_used)
            size = min(node_used - inner, grad.shape[0] - at)
            g_node[share, inner:inner + size, :] = grad[at:at + size, :].astype(BF16)
            at += size

    for j in range(GROUP):
        g_node[j, node_used:, :] = jnp.zeros((TILE - node_used, features), BF16)
        ra_node[j, node_used:, :] = jnp.zeros((TILE - node_used, features), BF16)
    put_node_grads(0, dot_tn(ns[...], node_first_grad[...]))
    put_node_grads(features, dot_tn(agg_rows[...], node_first_grad[...]))
    put_node_grads(2 * features, dot_tn(node_hid[...], node_pre_grad[...]))
    start_a(0, g_node, ra_node, node_used)

    def node_base(i, carry):
        rows = rows_at(i, NODE_CHUNK)
        base[rows, :] = nc[rows, :].astype(F32) + dot_nt(node_first_grad[rows, :], nw1[:features, :])
        return carry

    lax.fori_loop(0, node_chunks, node_base, 0, unroll=UNROLL)

    node_forward(nf, own_f, wait_exchange(3), False)
    shift(1, new_nodes, o_nn, 1).start()

    all_a(0, g_node, ra_node, node_used).wait_recv()
    start_b(0, ra_node)

    operand(11).wait()
    table_g[own_tiles:] = wait_exchange(4).reshape(mirror_tiles, TILE, features)

    def edge_back(i, carry):
        s_first, s_pre, s_gain, s_shift = carry
        rows = rows_at(i, EDGE_CHUNK)
        from_recv = jnp.concatenate(
            [fetch(recv_hot, i * per_chunk + j, table_g, 1) for j in range(per_chunk)], axis=0
        )
        top = live_rows(i) * (ec[rows, :].astype(F32) + from_recv)
        normed = edge_norm[rows, :]
        pre_grad = norm_back(top * ev[2:3, :], normed, edge_inv[rows, :]).astype(BF16)
        first = jnp.where(edge_pre[rows, :] > 0.0, dot_nt(pre_grad, w2[...]), 0.0).astype(BF16)
        edge_pre_grad[rows, :] = pre_grad
        edge_first_grad[rows, :] = first
        to_send = dot_nt(first, w1[features:2 * features, :])
        to_recv = dot_nt(first, w1[2 * features:, :])
        for j in range(per_chunk):
            b = i * per_chunk + j
            block_sums[b] = block_sum(send_hot_t[b], b, to_send[j * TILE:(j + 1) * TILE, :])
            block_sums[blocks + b] = block_sum(recv_hot_t[b], b, to_recv[j * TILE:(j + 1) * TILE, :])
        return (
            s_first + col_sum(first.astype(F32)),
            s_pre + col_sum(pre_grad.astype(F32)),
            s_gain + col_sum(top * normed),
            s_shift + col_sum(top),
        )

    sums = lax.fori_loop(0, edge_chunks, edge_back, (zero_row,) * 4, unroll=UNROLL)
    for j in range(4):
        vec[j:j + 1, :] = sums[j]
    send_mirror_sums(5, 0, 2 * blocks)

    va[apos] = vec[...]
    for k in range(1, GROUP):
        other, device = a_partner(k)
        pltpu.make_async_remote_copy(
            vec, va.at[apos], v_s.at[0], v_r.at[0], device_id={"dom": device}, device_id_type=MESH
        ).start()

    for part, rows in enumerate((es, sent_rows, recv_rows)):
        grad = dot_tn(rows[...], edge_first_grad[...]).astype(BF16)
        g_edge[2 * part] = grad[:TILE, :]
        g_edge[2 * part + 1] = grad[TILE:, :]
    grad = dot_tn(edge_hid[...], edge_pre_grad[...]).astype(BF16)
    g_edge[6] = grad[:TILE, :]
    g_edge[7] = grad[TILE:, :]
    start_a(1, g_edge, ra_edge, TILE)

    def edge_out(i, carry):
        rows = rows_at(i, EDGE_CHUNK)
        old_edges[rows, :] = (
            ec[rows, :].astype(F32) + dot_nt(edge_first_grad[rows, :], w1[:features, :])
        ).astype(BF16)
        return carry

    lax.fori_loop(0, edge_chunks, edge_out, 0, unroll=UNROLL)
    shift(2, old_edges, o_pe, phase_count - 1).start()

    own_sums(own_s, 0, 2 * blocks)
    all_b(0).wait_recv()
    start_gather_b(0)
    all_a(1, g_edge, ra_edge, TILE).wait_recv()
    start_b(1, ra_edge)

    returned = wait_exchange(5)

    def node_out(i, carry):
        rows = rows_at(i, NODE_CHUNK)
        old_nodes[rows, :] = (
            base[rows, :] + own_s[rows, :] + dot(want_hot_t[rows, :], returned)
        ).astype(BF16)
        shift(3, old_nodes.at[rows, :], o_pn.at[rows, :], phase_count - 1).start()
        return carry

    lax.fori_loop(0, node_chunks, node_out, 0, unroll=UNROLL)

    all_b(1).wait_recv()
    start_gather_b(1)
    all_gather_b(0).wait_recv()
    start_gather_a(0, o_gn)

    group_part = pl.ds(0, GROUP - 1)
    first_all = pltpu.make_async_remote_copy(
        va.at[group_part], va.at[group_part], v_s.at[0], v_r.at[0],
        device_id={"dom": a_partner(1)[1]}, device_id_type=MESH,
    )
    first_all.wait_recv()
    first_all.wait_send()
    total = va[0]
    for k in range(1, GROUP):
        total = total + va[k]
    vec[...] = total
    vb[zpos] = total
    for k in range(1, Z_SIZE):
        other, device = b_partner(k)
        pltpu.make_async_remote_copy(
            vec, vb.at[zpos], v_s.at[1], v_r.at[1], device_id={"dom": device}, device_id_type=MESH
        ).start()

    all_gather_b(1).wait_recv()
    start_gather_a(1, o_ge)
    second_all = pltpu.make_async_remote_copy(
        vb.at[group_part], vb.at[group_part], v_s.at[1], v_r.at[1],
        device_id={"dom": b_partner(1)[1]}, device_id_type=MESH,
    )
    second_all.wait_recv()
    total = vb[0]
    for k in range(1, Z_SIZE):
        total = total + vb[k]
    o_gv[...] = total

    for x in range(6):
        exchange_all(x).wait_send()
    all_a(0, g_node, ra_node, node_used).wait_send()
    all_a(1, g_edge, ra_edge, TILE).wait_send()
    second_all.wait_send()
    for which, out in ((0, o_gn), (1, o_ge)):
        all_b(which).wait_send()
        all_gather_b(which).wait_send()
        pltpu.make_async_copy(ab.at[which], out.at[apos], local_sem.at[which]).wait()
        all_gather_a(which, out).wait_send()
        all_gather_a(which, out).wait_recv()
    shift(0, new_edges, o_ne, 1).wait()
    shift(1, new_nodes, o_nn, 1).wait()
    shift(2, old_edges, o_pe, phase_count - 1).wait()
    shift(3, old_nodes, o_pn, phase_count - 1).wait()


def tick(dom_count, phase_count, *arrays):
    edge_dev, features = arrays[0].shape
    node_dev = arrays[1].shape[0]
    blocks = edge_dev // TILE
    slots = node_dev + dom_count * 8
    vmem = lambda shape, kind=BF16: pltpu.VMEM(shape, kind)
    sem = lambda count: pltpu.SemaphoreType.DMA((count,))
    mirror_tiles = dom_count * 8 // TILE
    scratch = (
        [vmem(a.shape, a.dtype) for a in arrays[:12]]
        + [vmem((mirror_tiles, 8, TILE), F32)]
        + [vmem((blocks, TILE, TILE))] * 4
        + [vmem((dom_count * 8, node_dev)), vmem((node_dev, dom_count * 8))]
        + [vmem((slots // TILE, TILE, features))] * 3
        + [vmem((6, dom_count, 16, 128))] * 2
        + [vmem((edge_dev, features))] * 2
        + [vmem((edge_dev, features), F32), vmem((edge_dev, features)), vmem((edge_dev, features), F32), vmem((edge_dev, 1), F32)]
        + [vmem((edge_dev, features))] * 2
        + [vmem((node_dev, features), F32), vmem((node_dev, features)), vmem((node_dev, features), F32), vmem((node_dev, 1), F32)]
        + [vmem((node_dev, features))] * 3
        + [vmem((2 * blocks, TILE, features), F32)]
        + [vmem((node_dev, features), F32)] * 3
        + [vmem((edge_dev, features)), vmem((node_dev, features))] * 2
        + [vmem((GROUP, TILE, features))] * 4
        + [vmem((2, Z_SIZE, 16, features))] * 2
        + [vmem((2, 16, features)), vmem((2, Z_SIZE, 16, features))]
        + [vmem((GROUP, 8, features), F32), vmem((Z_SIZE, 8, features), F32), vmem((8, features), F32)]
        + [sem(6), sem(6), sem(4), sem(4)]
        + [sem(2)] * 11
        + [sem(12)]
    )
    in_hbm = pl.BlockSpec(memory_space=pltpu.HBM)
    in_vmem = pl.BlockSpec(memory_space=pltpu.VMEM)
    in_smem = pl.BlockSpec(memory_space=pltpu.SMEM)
    anywhere = pl.BlockSpec(memory_space=pl.ANY)
    out_shape = (
        jax.ShapeDtypeStruct((edge_dev, features), BF16),
        jax.ShapeDtypeStruct((node_dev, features), BF16),
        jax.ShapeDtypeStruct((edge_dev, features), BF16),
        jax.ShapeDtypeStruct((node_dev, features), BF16),
        jax.ShapeDtypeStruct((GROUP, Z_SIZE, 16, features), BF16),
        jax.ShapeDtypeStruct((GROUP, Z_SIZE, 16, features), BF16),
        jax.ShapeDtypeStruct((8, features), F32),
    )

    def kernel(*refs):
        tick_kernel(dom_count, phase_count, *refs)

    return pl.pallas_call(
        kernel,
        out_shape=out_shape,
        in_specs=[in_hbm] * 12 + [in_vmem] * 2 + [in_smem] * 2,
        out_specs=[anywhere] * 6 + [in_vmem],
        scratch_shapes=scratch,
        name="tick",
        compiler_params=pltpu.CompilerParams(
            collective_id=0, has_side_effects=True, vmem_limit_bytes=VMEM_BYTES
        ),
    )(*arrays)


def hand_over_kernel(
    ne, nn, pe, pn, ge, gn, gv,
    o_ne, o_nn, o_pe, o_pn, o_ew1, o_ew2, o_ev, o_nw1, o_nw2, o_nv,
    ew1, ew2, nw1, nw2, v_ne, v_nn, v_pe, v_pn, v_ge, v_gn, v_gv, in_sems, sems,
):
    features = gv.shape[1]
    arriving = [(gn, v_gn), (ge, v_ge), (gv, v_gv), (ne, v_ne), (nn, v_nn), (pe, v_pe), (pn, v_pn)]
    arriving = [pltpu.make_async_copy(src, dst, in_sems.at[n]) for n, (src, dst) in enumerate(arriving)]
    copies = [(v_ne, o_ne.at[0]), (v_nn, o_nn.at[0]), (v_pe, o_pe.at[0]), (v_pn, o_pn.at[0])]
    copies += [(v_gv.at[pl.ds(0, 4)], o_ev.at[0]), (v_gv.at[pl.ds(4, 4)], o_nv.at[0])]
    copies += [(ew1, o_ew1.at[0]), (ew2, o_ew2.at[0]), (nw1, o_nw1.at[0]), (nw2, o_nw2.at[0])]
    copies = [pltpu.make_async_copy(src, dst, sems.at[n]) for n, (src, dst) in enumerate(copies)]
    for copy in arriving:
        copy.start()
    arriving[0].wait()
    used = (3 * features) // GROUP
    cut = 2 * features
    for share in range(GROUP):
        rows = v_gn[share, 0:used // 16].reshape(used, features).astype(F32)
        first = share * used
        inner = min(max(cut - first, 0), used)
        if inner > 0:
            nw1[first:first + inner, :] = rows[:inner]
        if inner < used:
            nw2[first + inner - cut:first + used - cut, :] = rows[inner:]
    copies[8].start()
    copies[9].start()
    arriving[1].wait()
    ew1[...] = v_ge[0:6].reshape(3 * features, features).astype(F32)
    copies[6].start()
    ew2[...] = v_ge[6:8].reshape(features, features).astype(F32)
    copies[7].start()
    arriving[2].wait()
    copies[4].start()
    copies[5].start()
    for n in range(4):
        arriving[3 + n].wait()
        copies[n].start()
    for copy in copies:
        copy.wait()


def hand_over(ne, nn, pe, pn, ge, gn, gv):
    features = gv.shape[1]
    shape = lambda rows, kind: jax.ShapeDtypeStruct((1, rows, features), kind)
    out_shape = tuple(shape(a.shape[0], BF16) for a in (ne, nn, pe, pn)) + (
        shape(3 * features, F32), shape(features, F32), shape(4, F32),
        shape(2 * features, F32), shape(features, F32), shape(4, F32),
    )
    grads = [pltpu.VMEM((n * features, features), F32) for n in (3, 1, 2, 1)]
    held = [pltpu.VMEM(a.shape, a.dtype) for a in (ne, nn, pe, pn, ge, gn, gv)]
    in_hbm = pl.BlockSpec(memory_space=pltpu.HBM)
    return pl.pallas_call(
        hand_over_kernel,
        out_shape=out_shape,
        in_specs=[in_hbm] * 7,
        out_specs=[in_hbm] * 10,
        scratch_shapes=grads + held + [pltpu.SemaphoreType.DMA((7,)), pltpu.SemaphoreType.DMA((10,))],
        name="hand_over",
        compiler_params=pltpu.CompilerParams(vmem_limit_bytes=VMEM_BYTES),
    )(ne, nn, pe, pn, ge, gn, gv)


def on_device(
    edges_fwd, nodes_fwd, edges_stash, nodes_stash, edge_cot, node_cot,
    edge_w1, edge_w2, edge_vectors, node_w1, node_w2, node_vectors,
    edge_nodes, mirror_rows, edge_count,
):
    dom_count = lax.axis_size("dom")
    phase_count = lax.axis_size("phase")
    features = edges_fwd.shape[2]
    ne, nn, pe, pn, ge, gn, gv = tick(
        dom_count, phase_count,
        edges_fwd[0], nodes_fwd[0], edges_stash[0], nodes_stash[0], edge_cot[0], node_cot[0],
        edge_w1[0], edge_w2[0], edge_vectors[0], node_w1[0], node_w2[0], node_vectors[0],
        edge_nodes, mirror_rows[0].T, edge_nodes, edge_count,
    )
    return hand_over(ne, nn, pe, pn, ge, gn, gv)


def solution(mesh):
    rows = P("phase", "dom", None)
    whole = P("phase", None, None)
    in_specs = (rows,) * 6 + (whole,) * 6 + (P(None, "dom"), P("dom", None, None), P("dom"))
    out_specs = (rows,) * 4 + (whole,) * 6
    return jax.shard_map(
        on_device, mesh=mesh, in_specs=in_specs, out_specs=out_specs, check_vma=False
    )
```

```python
import jax
import jax.numpy as jnp
from jax import lax
from jax.experimental import pallas as pl
from jax.experimental.pallas import tpu as pltpu
from jax.sharding import PartitionSpec as P

TILE = 128
EPSILON = 1e-05
Z_SIZE = 8
GROUP = 8
F32 = jnp.float32
BF16 = jnp.bfloat16
MESH = pl.DeviceIdType.MESH
EDGE_CHUNK = 768
NODE_CHUNK = 1024
UNROLL = False
A_ORDER = (4, 5, 3, 6, 2, 7, 1)
B_ORDER = (4, 3, 5, 2, 6, 1, 7)
OUT_CHUNK = 256
VMEM_BYTES = 63 * 2**20


def dot(a, b, contract=((1,), (0,))):
    return lax.dot_general(a, b, (contract, ((), ())), preferred_element_type=F32)


def dot_nt(a, b):
    return dot(a, b, ((1,), (1,)))


def dot_tn(a, b):
    return dot(a, b, ((0,), (0,)))


def layer_norm(pre_norm):
    row_mean = jnp.mean(pre_norm, axis=-1, keepdims=True)
    centered = pre_norm - row_mean
    row_var = jnp.mean(centered * centered, axis=-1, keepdims=True)
    inverse = lax.rsqrt(row_var + EPSILON)
    return centered * inverse, inverse


def norm_back(scaled, normed, inverse):
    mean_first = jnp.mean(scaled, axis=-1, keepdims=True)
    mean_second = jnp.mean(scaled * normed, axis=-1, keepdims=True)
    return inverse * (scaled - mean_first - normed * mean_second)


def to_slabs(rows):
    count = rows.shape[0] // 8
    left = rows[:, :128].reshape(count, 8, 128)
    right = rows[:, 128:].reshape(count, 8, 128)
    return jnp.concatenate([left, right], axis=1).astype(BF16)


def from_slabs(slabs):
    wide = slabs.astype(F32)
    count = wide.shape[0]
    left = wide[:, :8, :].reshape(count * 8, 128)
    right = wide[:, 8:, :].reshape(count * 8, 128)
    return jnp.concatenate([left, right], axis=1).astype(BF16)


def col_sum(rows):
    return jnp.sum(rows, axis=0, keepdims=True)


def rows_at(i, size):
    return pl.ds(pl.multiple_of(i * size, size), size)


def tick_kernel(
    dom_count,
    phase_count,
    h_ef, h_nf, h_es, h_ns, h_ec, h_nc, h_w1, h_w2, h_ev, h_nw1, h_nw2, h_nv, ends, mirror, s_ends, cnt,
    o_ne, o_nn, o_pe, o_pn, o_ge, o_gn, o_gv,
    ef, nf, es, ns, ec, nc, w1, w2, ev, nw1, nw2, nv, want_row,
    send_hot, send_hot_t, recv_hot, recv_hot_t, want_hot, want_hot_t,
    table_s, table_f, table_g, out_slab, in_slab,
    sent_rows, recv_rows, edge_pre, edge_hid, edge_norm, edge_inv, edge_pre_grad, edge_first_grad,
    node_pre, node_hid, node_norm, node_inv, agg_rows, node_first_grad, node_pre_grad,
    block_sums, own_s, own_f, base,
    new_edges, new_nodes, old_edges, old_nodes,
    g_edge, g_node, ra_edge, ra_node, sb, rb, fb, ab, va, vb, vec,
    x_send, x_recv, sh_send, sh_recv, ra_s, ra_r, rb_s, rb_r, gb_s, gb_r, ga_s, ga_r, v_s, v_r, local_sem, in_sem,
):
    me = lax.axis_index("dom")
    phase = lax.axis_index("phase")
    zpos = lax.rem(me // 2, Z_SIZE)
    apos = (me // (2 * Z_SIZE)) * 2 + lax.rem(me, 2)
    features = ef.shape[1]
    node_dev = nf.shape[0]
    edge_dev = ef.shape[0]
    blocks = edge_dev // TILE
    own_tiles = node_dev // TILE
    mirror_tiles = (dom_count * 8) // TILE
    node_chunks = node_dev // NODE_CHUNK
    edge_chunks = edge_dev // EDGE_CHUNK
    per_chunk = EDGE_CHUNK // TILE

    def a_partner(k):
        other = lax.rem(apos + k, GROUP)
        return other, (other // 2) * (2 * Z_SIZE) + zpos * 2 + lax.rem(other, 2)

    def b_partner(k):
        other = lax.rem(zpos + k, Z_SIZE)
        return other, me + 2 * (other - zpos)

    operands = [
        (h_ns, ns), (h_nf, nf), (h_es, es), (h_w1, w1), (h_w2, w2), (h_ev, ev), (h_ef, ef),
        (h_nw1, nw1), (h_nw2, nw2), (h_nv, nv), (h_nc, nc), (h_ec, ec),
    ]

    def operand(n):
        return pltpu.make_async_copy(operands[n][0], operands[n][1], in_sem.at[n])

    for n in range(len(operands)):
        operand(n).start()

    barrier = pltpu.get_barrier_semaphore()

    def greet(k, carry):
        pl.semaphore_signal(
            barrier, inc=1, device_id={"dom": lax.rem(me + k, dom_count)}, device_id_type=MESH
        )
        return carry

    lax.fori_loop(1, dom_count, greet, 0)
    for step in (1, phase_count - 1):
        pl.semaphore_signal(
            barrier, inc=1, device_id={"phase": lax.rem(phase + step, phase_count)}, device_id_type=MESH
        )

    groups = dom_count // (2 * Z_SIZE)
    ypos = me // (2 * Z_SIZE)

    def swing(n, size):
        return size // 2 + (1 - 2 * lax.rem(n, 2)) * ((n + 1) // 2)

    def start_exchange(x):
        def one(k, carry):
            other = (
                lax.rem(ypos + swing(lax.rem(k // 2, groups), groups), groups) * (2 * Z_SIZE)
                + lax.rem(zpos + swing(k // (2 * groups), Z_SIZE), Z_SIZE) * 2
                + lax.rem(me + 1 + k, 2)
            )
            pltpu.make_async_remote_copy(
                out_slab.at[x, other], in_slab.at[x, me], x_send.at[x], x_recv.at[x],
                device_id={"dom": other}, device_id_type=MESH,
            ).start()
            return carry

        lax.fori_loop(0, dom_count - 1, one, 0)
        in_slab[x, me] = out_slab[x, me]

    def exchange_all(x):
        part = pl.ds(0, dom_count - 1)
        return pltpu.make_async_remote_copy(
            out_slab.at[x, part], in_slab.at[x, part], x_send.at[x], x_recv.at[x],
            device_id={"dom": lax.rem(me + 1, dom_count)}, device_id_type=MESH,
        )

    def wait_exchange(x):
        exchange_all(x).wait_recv()
        return from_slabs(in_slab[x])

    def shift(slot, src, dst, step):
        return pltpu.make_async_remote_copy(
            src, dst, sh_send.at[slot], sh_recv.at[slot],
            device_id={"phase": lax.rem(phase + step, phase_count)}, device_id_type=MESH,
        )

    sub_iota = lax.broadcasted_iota(jnp.int32, (TILE, TILE), 0)
    lane_iota = lax.broadcasted_iota(jnp.int32, (TILE, TILE), 1)

    slab_iota = lax.broadcasted_iota(jnp.int32, (TILE, dom_count), 0)
    dom_iota = lax.broadcasted_iota(jnp.int32, (TILE, dom_count), 1)
    in_slab_iota = lax.broadcasted_iota(jnp.int32, (TILE, 8), 0)
    cap_iota = lax.broadcasted_iota(jnp.int32, (TILE, 8), 1)
    lane_float = lane_iota.astype(F32)
    sub_float = sub_iota.astype(F32)
    mirror_high = lax.div(mirror[...], 8).astype(F32).astype(BF16)
    mirror_low = lax.rem(mirror[...], 8).astype(F32).astype(BF16)

    def build_want(b, carry):
        owner = (dom_iota == b * 16 + lax.div(slab_iota, 8)).astype(F32).astype(BF16)
        named = dot_nt(owner, mirror_high) * 8.0 + dot_nt(owner, mirror_low)
        named = jnp.where(cap_iota == lax.rem(in_slab_iota, 8), named, 0.0)
        col = jnp.broadcast_to(jnp.sum(named, axis=1, keepdims=True), (TILE, TILE))
        want_row[b] = jnp.transpose(col)[:8]
        for j in range(own_tiles):
            want_hot[rows_at(b, TILE), j * TILE:(j + 1) * TILE] = (col == lane_float + float(j * TILE)).astype(F32).astype(BF16)
        return carry

    lax.fori_loop(0, mirror_tiles, build_want, 0)

    def pick_rows(x, rows):
        out_slab[x] = to_slabs(dot(want_hot[...], rows))

    operand(0).wait()
    pick_rows(0, ns[...])
    pl.semaphore_wait(barrier, dom_count - 1 + 2)
    start_exchange(0)
    operand(1).wait()
    pick_rows(1, nf[...])
    start_exchange(1)

    def build_edges(b, carry):
        for end, hot, hot_t in ((0, send_hot, send_hot_t), (1, recv_hot, recv_hot_t)):
            row = jnp.broadcast_to(jnp.bitwise_and(ends[end:end + 1, rows_at(b, TILE)], TILE - 1), (TILE, TILE))
            hot_t[b] = (row == sub_iota).astype(F32).astype(BF16)
            hot[b] = (jnp.transpose(row) == lane_iota).astype(F32).astype(BF16)
        return carry

    lax.fori_loop(0, blocks, build_edges, 0)

    for j in range(mirror_tiles):
        row = jnp.broadcast_to(want_row[j, 0:1, :], (TILE, TILE))
        for i in range(own_tiles):
            want_hot_t[i * TILE:(i + 1) * TILE, j * TILE:(j + 1) * TILE] = (row == sub_float + float(i * TILE)).astype(F32).astype(BF16)

    table_s[0:own_tiles] = ns[...].reshape(own_tiles, TILE, features)
    table_f[0:own_tiles] = nf[...].reshape(own_tiles, TILE, features)

    def fetch(hot, b, table, end):
        return dot(hot[b], table[lax.div(s_ends[end, b * TILE], TILE)])

    def live_rows(i):
        at = lax.broadcasted_iota(jnp.int32, (EDGE_CHUNK, features), 0) + i * EDGE_CHUNK
        return jnp.where(at < cnt[0], 1.0, 0.0).astype(F32)

    def block_sum(hot_t, b, rows):
        high = rows.astype(BF16)
        low = (rows - high.astype(F32)).astype(BF16)
        return dot(jnp.concatenate([hot_t, hot_t], axis=1), jnp.concatenate([high, low], axis=0))

    def tile_total(k, first, count):
        total = jnp.zeros((TILE, features), F32)
        for b in range(count):
            end, block = divmod(first + b, blocks)
            tile = lax.div(ends[end:end + 1, block * TILE:block * TILE + 1], TILE)
            chosen = (tile == k).astype(F32)
            total = total + jnp.broadcast_to(chosen, (TILE, features)) * block_sums[b]
        return total

    def put_mirror_sums(x, first, count):
        def one(q, carry):
            total = tile_total(own_tiles + q, first, count)
            out_slab[x, pl.ds(pl.multiple_of(q * 16, 16), 16)] = to_slabs(total)
            return carry

        lax.fori_loop(0, mirror_tiles, one, 0)

    def own_sums(own, first, count):
        def one(k, carry):
            own[rows_at(k, TILE), :] = tile_total(k, first, count)
            return carry

        lax.fori_loop(0, own_tiles, one, 0)

    def edge_start(edges):
        edge_pre[...] = dot(edges[...], w1[:features, :]) + ev[0:1, :]

    def node_start(nodes):
        node_pre[...] = dot(nodes[...], nw1[:features, :]) + nv[0:1, :]

    def edge_forward(edges, table, keep):
        def one(i, carry):
            rows = rows_at(i, EDGE_CHUNK)
            from_send = jnp.concatenate(
                [fetch(send_hot, i * per_chunk + j, table, 0) for j in range(per_chunk)], axis=0
            ).astype(BF16)
            from_recv = jnp.concatenate(
                [fetch(recv_hot, i * per_chunk + j, table, 1) for j in range(per_chunk)], axis=0
            ).astype(BF16)
            stacked = jnp.concatenate([from_send, from_recv], axis=1)
            if keep:
                pre = edge_pre[rows, :] + dot(stacked, w1[features:, :])
            else:
                pre = dot(edges[rows, :], w1[:features, :]) + dot(stacked, w1[features:, :]) + ev[0:1, :]
            hidden = jnp.maximum(pre, 0.0).astype(BF16)
            normed, inverse = layer_norm(dot(hidden, w2[...]) + ev[1:2, :])
            message = live_rows(i) * (normed * ev[2:3, :] + ev[3:4, :])
            if keep:
                sent_rows[rows, :] = from_send
                recv_rows[rows, :] = from_recv
                edge_pre[rows, :] = pre
                edge_hid[rows, :] = hidden
                edge_norm[rows, :] = normed
                edge_inv[rows, :] = inverse
            else:
                new_edges[rows, :] = (edges[rows, :].astype(F32) + message).astype(BF16)
            for j in range(per_chunk):
                b = i * per_chunk + j
                block_sums[b] = block_sum(recv_hot_t[b], b, message[j * TILE:(j + 1) * TILE, :])
            return carry

        lax.fori_loop(0, edge_chunks, one, 0, unroll=UNROLL)

    def node_forward(nodes, own, returned, keep):
        def one(i, carry):
            rows = rows_at(i, NODE_CHUNK)
            total = own[rows, :] + dot(want_hot_t[rows, :], returned)
            gathered = total.astype(BF16)
            if keep:
                pre = node_pre[rows, :] + dot(gathered, nw1[features:, :])
            else:
                stacked = jnp.concatenate([nodes[rows, :], gathered], axis=1)
                pre = dot(stacked, nw1[...]) + nv[0:1, :]
            hidden = jnp.maximum(pre, 0.0).astype(BF16)
            normed, inverse = layer_norm(dot(hidden, nw2[...]) + nv[1:2, :])
            if keep:
                agg_rows[rows, :] = gathered
                node_pre[rows, :] = pre
                node_hid[rows, :] = hidden
                node_norm[rows, :] = normed
                node_inv[rows, :] = inverse
            else:
                new_nodes[rows, :] = (
                    nodes[rows, :].astype(F32) + (normed * nv[2:3, :] + nv[3:4, :])
                ).astype(BF16)
            return carry

        lax.fori_loop(0, node_chunks, one, 0, unroll=UNROLL)

    for n in (2, 3, 4, 5):
        operand(n).wait()
    edge_start(es)
    table_s[own_tiles:] = wait_exchange(0).reshape(mirror_tiles, TILE, features)
    edge_forward(es, table_s, True)
    put_mirror_sums(2, blocks, blocks)
    start_exchange(2)
    own_sums(own_s, blocks, blocks)

    operand(6).wait()
    table_f[own_tiles:] = wait_exchange(1).reshape(mirror_tiles, TILE, features)
    edge_forward(ef, table_f, False)
    shift(0, new_edges, o_ne, 1).start()
    put_mirror_sums(3, blocks, blocks)
    start_exchange(3)
    own_sums(own_f, blocks, blocks)

    for n in (7, 8, 9, 10):
        operand(n).wait()
    node_start(ns)
    returned = wait_exchange(2)
    node_forward(ns, own_s, returned, True)

    def node_back(i, carry):
        s_first, s_pre, s_gain, s_shift = carry
        rows = rows_at(i, NODE_CHUNK)
        top = nc[rows, :].astype(F32)
        normed = node_norm[rows, :]
        pre_grad = norm_back(top * nv[2:3, :], normed, node_inv[rows, :]).astype(BF16)
        first = jnp.where(node_pre[rows, :] > 0.0, dot_nt(pre_grad, nw2[...]), 0.0).astype(BF16)
        node_pre_grad[rows, :] = pre_grad
        node_first_grad[rows, :] = first
        table_g[rows_at(i, NODE_CHUNK // TILE)] = dot_nt(first, nw1[features:, :]).astype(BF16).reshape(NODE_CHUNK // TILE, TILE, features)
        return (
            s_first + col_sum(first.astype(F32)),
            s_pre + col_sum(pre_grad.astype(F32)),
            s_gain + col_sum(top * normed),
            s_shift + col_sum(top),
        )

    zero_row = jnp.zeros((1, features), F32)
    sums = lax.fori_loop(0, node_chunks, node_back, (zero_row,) * 4, unroll=UNROLL)
    for j in range(4):
        vec[4 + j:5 + j, :] = sums[j]

    pick_rows(4, table_g[0:own_tiles].reshape(node_dev, features))
    start_exchange(4)

    def start_a(which, grads, arrived, used):
        arrived[apos] = grads[apos]
        for k in A_ORDER:
            other, device = a_partner(k)
            pltpu.make_async_remote_copy(
                grads.at[other, pl.ds(0, used)], arrived.at[apos, pl.ds(0, used)],
                ra_s.at[which], ra_r.at[which], device_id={"dom": device}, device_id_type=MESH,
            ).start()

    def all_a(which, grads, arrived, used):
        part = pl.ds(0, GROUP - 1)
        return pltpu.make_async_remote_copy(
            grads.at[part, pl.ds(0, used)], arrived.at[part, pl.ds(0, used)],
            ra_s.at[which], ra_r.at[which], device_id={"dom": a_partner(1)[1]}, device_id_type=MESH,
        )

    def start_b(which, arrived):
        total = arrived[0].astype(F32)
        for k in range(1, GROUP):
            total = total + arrived[k].astype(F32)
        sb[which] = total.astype(BF16).reshape(Z_SIZE, 16, features)
        rb[which, zpos] = sb[which, zpos]
        for k in B_ORDER:
            other, device = b_partner(k)
            pltpu.make_async_remote_copy(
                sb.at[which, other], rb.at[which, zpos], rb_s.at[which], rb_r.at[which],
                device_id={"dom": device}, device_id_type=MESH,
            ).start()

    def all_b(which):
        part = pl.ds(0, Z_SIZE - 1)
        return pltpu.make_async_remote_copy(
            sb.at[which, part], rb.at[which, part], rb_s.at[which], rb_r.at[which],
            device_id={"dom": b_partner(1)[1]}, device_id_type=MESH,
        )

    def start_gather_b(which):
        total = rb[which, 0].astype(F32)
        for k in range(1, Z_SIZE):
            total = total + rb[which, k].astype(F32)
        fb[which] = total.astype(BF16)
        ab[which, zpos] = fb[which]
        for k in B_ORDER:
            other, device = b_partner(k)
            pltpu.make_async_remote_copy(
                fb.at[which], ab.at[which, zpos], gb_s.at[which], gb_r.at[which],
                device_id={"dom": device}, device_id_type=MESH,
            ).start()

    def all_gather_b(which):
        part = pl.ds(0, Z_SIZE - 1)
        return pltpu.make_async_remote_copy(
            ab.at[which, part], ab.at[which, part], gb_s.at[which], gb_r.at[which],
            device_id={"dom": b_partner(1)[1]}, device_id_type=MESH,
        )

    z_used = ((3 * features) // GROUP // 16, Z_SIZE)

    def own_share(which, out):
        part = pl.ds(0, z_used[which])
        return pltpu.make_async_copy(ab.at[which, part], out.at[apos, part], local_sem.at[which])

    def start_gather_a(which, out):
        part = pl.ds(0, z_used[which])
        own_share(which, out).start()
        for k in A_ORDER:
            other, device = a_partner(k)
            pltpu.make_async_remote_copy(
                ab.at[which, part], out.at[apos, part], ga_s.at[which], ga_r.at[which],
                device_id={"dom": device}, device_id_type=MESH,
            ).start()

    def all_gather_a(which, out):
        part = pl.ds(0, GROUP - 1)
        used = pl.ds(0, z_used[which])
        return pltpu.make_async_remote_copy(
            out.at[part, used], out.at[part, used], ga_s.at[which], ga_r.at[which],
            device_id={"dom": a_partner(1)[1]}, device_id_type=MESH,
        )

    node_used = (3 * features) // GROUP

    def put_node_grads(first_row, grad):
        at = 0
        while at < grad.shape[0]:
            share, inner = divmod(first_row + at, node_used)
            size = min(node_used - inner, grad.shape[0] - at)
            g_node[share, inner:inner + size, :] = grad[at:at + size, :].astype(BF16)
            at += size

    for j in range(GROUP):
        g_node[j, node_used:, :] = jnp.zeros((TILE - node_used, features), BF16)
        ra_node[j, node_used:, :] = jnp.zeros((TILE - node_used, features), BF16)
    put_node_grads(0, dot_tn(ns[...], node_first_grad[...]))
    put_node_grads(features, dot_tn(agg_rows[...], node_first_grad[...]))
    put_node_grads(2 * features, dot_tn(node_hid[...], node_pre_grad[...]))
    start_a(0, g_node, ra_node, node_used)

    def node_base(i, carry):
        rows = rows_at(i, NODE_CHUNK)
        base[rows, :] = nc[rows, :].astype(F32) + dot_nt(node_first_grad[rows, :], nw1[:features, :])
        return carry

    lax.fori_loop(0, node_chunks, node_base, 0, unroll=UNROLL)

    node_forward(nf, own_f, wait_exchange(3), False)
    shift(1, new_nodes, o_nn, 1).start()

    all_a(0, g_node, ra_node, node_used).wait_recv()
    start_b(0, ra_node)

    operand(11).wait()
    table_g[own_tiles:] = wait_exchange(4).reshape(mirror_tiles, TILE, features)

    def edge_back(i, carry):
        s_first, s_pre, s_gain, s_shift = carry
        rows = rows_at(i, EDGE_CHUNK)
        from_recv = jnp.concatenate(
            [fetch(recv_hot, i * per_chunk + j, table_g, 1) for j in range(per_chunk)], axis=0
        )
        top = live_rows(i) * (ec[rows, :].astype(F32) + from_recv)
        normed = edge_norm[rows, :]
        pre_grad = norm_back(top * ev[2:3, :], normed, edge_inv[rows, :]).astype(BF16)
        first = jnp.where(edge_pre[rows, :] > 0.0, dot_nt(pre_grad, w2[...]), 0.0).astype(BF16)
        edge_pre_grad[rows, :] = pre_grad
        edge_first_grad[rows, :] = first
        to_send = dot_nt(first, w1[features:2 * features, :])
        to_recv = dot_nt(first, w1[2 * features:, :])
        for j in range(per_chunk):
            b = i * per_chunk + j
            block_sums[b] = block_sum(send_hot_t[b], b, to_send[j * TILE:(j + 1) * TILE, :])
            block_sums[blocks + b] = block_sum(recv_hot_t[b], b, to_recv[j * TILE:(j + 1) * TILE, :])
        return (
            s_first + col_sum(first.astype(F32)),
            s_pre + col_sum(pre_grad.astype(F32)),
            s_gain + col_sum(top * normed),
            s_shift + col_sum(top),
        )

    sums = lax.fori_loop(0, edge_chunks, edge_back, (zero_row,) * 4, unroll=UNROLL)
    for j in range(4):
        vec[j:j + 1, :] = sums[j]
    for part, rows in enumerate((es, sent_rows, recv_rows)):
        grad = dot_tn(rows[...], edge_first_grad[...]).astype(BF16)
        g_edge[2 * part] = grad[:TILE, :]
        g_edge[2 * part + 1] = grad[TILE:, :]
    grad = dot_tn(edge_hid[...], edge_pre_grad[...]).astype(BF16)
    g_edge[6] = grad[:TILE, :]
    g_edge[7] = grad[TILE:, :]
    start_a(1, g_edge, ra_edge, TILE)

    put_mirror_sums(5, 0, 2 * blocks)
    start_exchange(5)

    def edge_out(i, carry):
        rows = rows_at(i, EDGE_CHUNK)
        old_edges[rows, :] = (
            ec[rows, :].astype(F32) + dot_nt(edge_first_grad[rows, :], w1[:features, :])
        ).astype(BF16)
        return carry

    lax.fori_loop(0, edge_chunks, edge_out, 0, unroll=UNROLL)
    shift(2, old_edges, o_pe, phase_count - 1).start()

    all_b(0).wait_recv()
    start_gather_b(0)

    va[apos] = vec[...]
    for k in range(1, GROUP):
        other, device = a_partner(k)
        pltpu.make_async_remote_copy(
            vec, va.at[apos], v_s.at[0], v_r.at[0], device_id={"dom": device}, device_id_type=MESH
        ).start()

    own_sums(own_s, 0, 2 * blocks)
    all_gather_b(0).wait_recv()
    start_gather_a(0, o_gn)
    all_a(1, g_edge, ra_edge, TILE).wait_recv()
    start_b(1, ra_edge)

    returned = wait_exchange(5)

    for i in range(node_dev // OUT_CHUNK):
        rows = pl.ds(i * OUT_CHUNK, OUT_CHUNK)
        old_nodes[rows, :] = (base[rows, :] + own_s[rows, :] + dot(want_hot_t[rows, :], returned)).astype(BF16)
        shift(3, old_nodes.at[rows, :], o_pn.at[rows, :], phase_count - 1).start()

    all_b(1).wait_recv()
    start_gather_b(1)
    group_part = pl.ds(0, GROUP - 1)
    first_all = pltpu.make_async_remote_copy(
        va.at[group_part], va.at[group_part], v_s.at[0], v_r.at[0],
        device_id={"dom": a_partner(1)[1]}, device_id_type=MESH,
    )
    first_all.wait_recv()
    first_all.wait_send()
    total = va[0]
    for k in range(1, GROUP):
        total = total + va[k]
    vec[...] = total
    vb[zpos] = total
    for k in range(1, Z_SIZE):
        other, device = b_partner(k)
        pltpu.make_async_remote_copy(
            vec, vb.at[zpos], v_s.at[1], v_r.at[1], device_id={"dom": device}, device_id_type=MESH
        ).start()

    all_gather_b(1).wait_recv()
    start_gather_a(1, o_ge)
    second_all = pltpu.make_async_remote_copy(
        vb.at[group_part], vb.at[group_part], v_s.at[1], v_r.at[1],
        device_id={"dom": b_partner(1)[1]}, device_id_type=MESH,
    )
    second_all.wait_recv()
    total = vb[0]
    for k in range(1, Z_SIZE):
        total = total + vb[k]
    o_gv[...] = total

    for x in range(6):
        exchange_all(x).wait_send()
    all_a(0, g_node, ra_node, node_used).wait_send()
    all_a(1, g_edge, ra_edge, TILE).wait_send()
    second_all.wait_send()
    for which, out in ((0, o_gn), (1, o_ge)):
        all_b(which).wait_send()
        all_gather_b(which).wait_send()
        own_share(which, out).wait()
        all_gather_a(which, out).wait_send()
        all_gather_a(which, out).wait_recv()
    shift(0, new_edges, o_ne, 1).wait()
    shift(1, new_nodes, o_nn, 1).wait()
    shift(2, old_edges, o_pe, phase_count - 1).wait()
    shift(3, old_nodes, o_pn, phase_count - 1).wait()


def tick(dom_count, phase_count, *arrays):
    edge_dev, features = arrays[0].shape
    node_dev = arrays[1].shape[0]
    blocks = edge_dev // TILE
    slots = node_dev + dom_count * 8
    vmem = lambda shape, kind=BF16: pltpu.VMEM(shape, kind)
    sem = lambda count: pltpu.SemaphoreType.DMA((count,))
    mirror_tiles = dom_count * 8 // TILE
    scratch = (
        [vmem(a.shape, a.dtype) for a in arrays[:12]]
        + [vmem((mirror_tiles, 8, TILE), F32)]
        + [vmem((blocks, TILE, TILE))] * 4
        + [vmem((dom_count * 8, node_dev)), vmem((node_dev, dom_count * 8))]
        + [vmem((slots // TILE, TILE, features))] * 3
        + [vmem((6, dom_count, 16, 128))] * 2
        + [vmem((edge_dev, features))] * 2
        + [vmem((edge_dev, features), F32), vmem((edge_dev, features)), vmem((edge_dev, features), F32), vmem((edge_dev, 1), F32)]
        + [vmem((edge_dev, features))] * 2
        + [vmem((node_dev, features), F32), vmem((node_dev, features)), vmem((node_dev, features), F32), vmem((node_dev, 1), F32)]
        + [vmem((node_dev, features))] * 3
        + [vmem((2 * blocks, TILE, features), F32)]
        + [vmem((node_dev, features), F32)] * 3
        + [vmem((edge_dev, features)), vmem((node_dev, features))] * 2
        + [vmem((GROUP, TILE, features))] * 4
        + [vmem((2, Z_SIZE, 16, features))] * 2
        + [vmem((2, 16, features)), vmem((2, Z_SIZE, 16, features))]
        + [vmem((GROUP, 8, features), F32), vmem((Z_SIZE, 8, features), F32), vmem((8, features), F32)]
        + [sem(6), sem(6), sem(4), sem(4)]
        + [sem(2)] * 11
        + [sem(12)]
    )
    in_hbm = pl.BlockSpec(memory_space=pltpu.HBM)
    in_vmem = pl.BlockSpec(memory_space=pltpu.VMEM)
    in_smem = pl.BlockSpec(memory_space=pltpu.SMEM)
    anywhere = pl.BlockSpec(memory_space=pl.ANY)
    out_shape = (
        jax.ShapeDtypeStruct((edge_dev, features), BF16),
        jax.ShapeDtypeStruct((node_dev, features), BF16),
        jax.ShapeDtypeStruct((edge_dev, features), BF16),
        jax.ShapeDtypeStruct((node_dev, features), BF16),
        jax.ShapeDtypeStruct((GROUP, Z_SIZE, 16, features), BF16),
        jax.ShapeDtypeStruct((GROUP, Z_SIZE, 16, features), BF16),
        jax.ShapeDtypeStruct((8, features), F32),
    )

    def kernel(*refs):
        tick_kernel(dom_count, phase_count, *refs)

    return pl.pallas_call(
        kernel,
        out_shape=out_shape,
        in_specs=[in_hbm] * 12 + [in_vmem] * 2 + [in_smem] * 2,
        out_specs=[anywhere] * 6 + [in_vmem],
        scratch_shapes=scratch,
        name="tick",
        compiler_params=pltpu.CompilerParams(
            collective_id=0, has_side_effects=True, vmem_limit_bytes=VMEM_BYTES
        ),
    )(*arrays)


def hand_over_kernel(
    ne, nn, pe, pn, ge, gn, gv,
    o_ne, o_nn, o_pe, o_pn, o_ew1, o_ew2, o_ev, o_nw1, o_nw2, o_nv,
    ew1, ew2, nw1, nw2, v_ne, v_nn, v_pe, v_pn, v_ge, v_gn, v_gv, in_sems, sems,
):
    features = gv.shape[1]
    arriving = [(gn, v_gn), (ge, v_ge), (gv, v_gv), (ne, v_ne), (nn, v_nn), (pe, v_pe), (pn, v_pn)]
    arriving = [pltpu.make_async_copy(src, dst, in_sems.at[n]) for n, (src, dst) in enumerate(arriving)]
    copies = [(v_ne, o_ne.at[0]), (v_nn, o_nn.at[0]), (v_pe, o_pe.at[0]), (v_pn, o_pn.at[0])]
    copies += [(v_gv.at[pl.ds(0, 4)], o_ev.at[0]), (v_gv.at[pl.ds(4, 4)], o_nv.at[0])]
    copies += [(ew1, o_ew1.at[0]), (ew2, o_ew2.at[0]), (nw1, o_nw1.at[0]), (nw2, o_nw2.at[0])]
    copies = [pltpu.make_async_copy(src, dst, sems.at[n]) for n, (src, dst) in enumerate(copies)]
    for copy in arriving:
        copy.start()
    arriving[0].wait()
    used = (3 * features) // GROUP
    cut = 2 * features
    for share in range(GROUP):
        rows = v_gn[share, 0:used // 16].reshape(used, features).astype(F32)
        first = share * used
        inner = min(max(cut - first, 0), used)
        if inner > 0:
            nw1[first:first + inner, :] = rows[:inner]
        if inner < used:
            nw2[first + inner - cut:first + used - cut, :] = rows[inner:]
    copies[8].start()
    copies[9].start()
    arriving[1].wait()
    ew1[...] = v_ge[0:6].reshape(3 * features, features).astype(F32)
    copies[6].start()
    ew2[...] = v_ge[6:8].reshape(features, features).astype(F32)
    copies[7].start()
    arriving[2].wait()
    copies[4].start()
    copies[5].start()
    for n in range(4):
        arriving[3 + n].wait()
        copies[n].start()
    for copy in copies:
        copy.wait()


def hand_over(ne, nn, pe, pn, ge, gn, gv):
    features = gv.shape[1]
    shape = lambda rows, kind: jax.ShapeDtypeStruct((1, rows, features), kind)
    out_shape = tuple(shape(a.shape[0], BF16) for a in (ne, nn, pe, pn)) + (
        shape(3 * features, F32), shape(features, F32), shape(4, F32),
        shape(2 * features, F32), shape(features, F32), shape(4, F32),
    )
    grads = [pltpu.VMEM((n * features, features), F32) for n in (3, 1, 2, 1)]
    held = [pltpu.VMEM(a.shape, a.dtype) for a in (ne, nn, pe, pn, ge, gn, gv)]
    in_hbm = pl.BlockSpec(memory_space=pltpu.HBM)
    return pl.pallas_call(
        hand_over_kernel,
        out_shape=out_shape,
        in_specs=[in_hbm] * 7,
        out_specs=[in_hbm] * 10,
        scratch_shapes=grads + held + [pltpu.SemaphoreType.DMA((7,)), pltpu.SemaphoreType.DMA((10,))],
        name="hand_over",
        compiler_params=pltpu.CompilerParams(vmem_limit_bytes=VMEM_BYTES),
    )(ne, nn, pe, pn, ge, gn, gv)


def on_device(
    edges_fwd, nodes_fwd, edges_stash, nodes_stash, edge_cot, node_cot,
    edge_w1, edge_w2, edge_vectors, node_w1, node_w2, node_vectors,
    edge_nodes, mirror_rows, edge_count,
):
    dom_count = lax.axis_size("dom")
    phase_count = lax.axis_size("phase")
    features = edges_fwd.shape[2]
    ne, nn, pe, pn, ge, gn, gv = tick(
        dom_count, phase_count,
        edges_fwd[0], nodes_fwd[0], edges_stash[0], nodes_stash[0], edge_cot[0], node_cot[0],
        edge_w1[0], edge_w2[0], edge_vectors[0], node_w1[0], node_w2[0], node_vectors[0],
        edge_nodes, mirror_rows[0].T, edge_nodes, edge_count,
    )
    return hand_over(ne, nn, pe, pn, ge, gn, gv)


def solution(mesh):
    rows = P("phase", "dom", None)
    whole = P("phase", None, None)
    in_specs = (rows,) * 6 + (whole,) * 6 + (P(None, "dom"), P("dom", None, None), P("dom"))
    out_specs = (rows,) * 4 + (whole,) * 6
    return jax.shard_map(
        on_device, mesh=mesh, in_specs=in_specs, out_specs=out_specs, check_vma=False
    )
```

```python
import jax
import jax.numpy as jnp
from jax import lax
from jax.experimental import pallas as pl
from jax.experimental.pallas import tpu as pltpu
from jax.sharding import PartitionSpec as P

TILE = 128
EPSILON = 1e-05
Z_SIZE = 8
GROUP = 8
F32 = jnp.float32
BF16 = jnp.bfloat16
MESH = pl.DeviceIdType.MESH
EDGE_CHUNK = 768
NODE_CHUNK = 1024
UNROLL = False
A_ORDER = (4, 5, 3, 6, 2, 7, 1)
B_ORDER = (4, 3, 5, 2, 6, 1, 7)
OUT_CHUNK = 256
VMEM_BYTES = 63 * 2**20


def dot(a, b, contract=((1,), (0,))):
    return lax.dot_general(a, b, (contract, ((), ())), preferred_element_type=F32)


def dot_nt(a, b):
    return dot(a, b, ((1,), (1,)))


def dot_tn(a, b):
    return dot(a, b, ((0,), (0,)))


def layer_norm(pre_norm):
    row_mean = jnp.mean(pre_norm, axis=-1, keepdims=True)
    centered = pre_norm - row_mean
    row_var = jnp.mean(centered * centered, axis=-1, keepdims=True)
    inverse = lax.rsqrt(row_var + EPSILON)
    return centered * inverse, inverse


def norm_back(scaled, normed, inverse):
    mean_first = jnp.mean(scaled, axis=-1, keepdims=True)
    mean_second = jnp.mean(scaled * normed, axis=-1, keepdims=True)
    return inverse * (scaled - mean_first - normed * mean_second)


def to_slabs(rows):
    count = rows.shape[0] // 8
    left = rows[:, :128].reshape(count, 8, 128)
    right = rows[:, 128:].reshape(count, 8, 128)
    return jnp.concatenate([left, right], axis=1).astype(BF16)


def from_slabs(slabs):
    wide = slabs.astype(F32)
    count = wide.shape[0]
    left = wide[:, :8, :].reshape(count * 8, 128)
    right = wide[:, 8:, :].reshape(count * 8, 128)
    return jnp.concatenate([left, right], axis=1).astype(BF16)


def col_sum(rows):
    return jnp.sum(rows, axis=0, keepdims=True)


def rows_at(i, size):
    return pl.ds(pl.multiple_of(i * size, size), size)


def tick_kernel(
    dom_count,
    phase_count,
    h_ef, h_nf, h_es, h_ns, h_ec, h_nc, h_w1, h_w2, h_ev, h_nw1, h_nw2, h_nv, ends, mirror, s_ends, cnt,
    o_ne, o_nn, o_pe, o_pn, o_ge, o_gn, o_gv,
    ef, nf, es, ns, ec, nc, w1, w2, ev, nw1, nw2, nv, want_row,
    send_hot, send_hot_t, recv_hot, recv_hot_t, want_hot, want_hot_t,
    table_s, table_f, table_g, out_slab, in_slab,
    sent_rows, recv_rows, edge_pre, edge_hid, edge_norm, edge_inv, edge_pre_grad, edge_first_grad,
    node_pre, node_hid, node_norm, node_inv, agg_rows, node_first_grad, node_pre_grad,
    block_sums, own_s, own_f, base,
    new_edges, new_nodes, old_edges, old_nodes,
    g_edge, g_node, ra_edge, ra_node, sb, rb, fb, ab, va, vb, vec,
    x_send, x_recv, sh_send, sh_recv, ra_s, ra_r, rb_s, rb_r, gb_s, gb_r, ga_s, ga_r, v_s, v_r, local_sem, in_sem,
):
    me = lax.axis_index("dom")
    phase = lax.axis_index("phase")
    zpos = lax.rem(me // 2, Z_SIZE)
    apos = (me // (2 * Z_SIZE)) * 2 + lax.rem(me, 2)
    features = ef.shape[1]
    node_dev = nf.shape[0]
    edge_dev = ef.shape[0]
    blocks = edge_dev // TILE
    own_tiles = node_dev // TILE
    mirror_tiles = (dom_count * 8) // TILE
    node_chunks = node_dev // NODE_CHUNK
    edge_chunks = edge_dev // EDGE_CHUNK
    per_chunk = EDGE_CHUNK // TILE

    def a_partner(k):
        other = lax.rem(apos + k, GROUP)
        return other, (other // 2) * (2 * Z_SIZE) + zpos * 2 + lax.rem(other, 2)

    def b_partner(k):
        other = lax.rem(zpos + k, Z_SIZE)
        return other, me + 2 * (other - zpos)

    operands = [
        (h_ns, ns), (h_nf, nf), (h_es, es), (h_w1, w1), (h_w2, w2), (h_ev, ev), (h_ef, ef),
        (h_nw1, nw1), (h_nw2, nw2), (h_nv, nv), (h_nc, nc), (h_ec, ec),
    ]

    def operand(n):
        return pltpu.make_async_copy(operands[n][0], operands[n][1], in_sem.at[n])

    for n in range(len(operands)):
        operand(n).start()

    barrier = pltpu.get_barrier_semaphore()

    def greet(k, carry):
        pl.semaphore_signal(
            barrier, inc=1, device_id={"dom": lax.rem(me + k, dom_count)}, device_id_type=MESH
        )
        return carry

    lax.fori_loop(1, dom_count, greet, 0)
    for step in (1, phase_count - 1):
        pl.semaphore_signal(
            barrier, inc=1, device_id={"phase": lax.rem(phase + step, phase_count)}, device_id_type=MESH
        )

    groups = dom_count // (2 * Z_SIZE)
    ypos = me // (2 * Z_SIZE)

    def swing(n, size):
        return size // 2 + (1 - 2 * lax.rem(n, 2)) * ((n + 1) // 2)

    def start_exchange(x):
        def one(k, carry):
            other = (
                lax.rem(ypos + swing(lax.rem(k // 2, groups), groups), groups) * (2 * Z_SIZE)
                + lax.rem(zpos + swing(k // (2 * groups), Z_SIZE), Z_SIZE) * 2
                + lax.rem(me + 1 + k, 2)
            )
            pltpu.make_async_remote_copy(
                out_slab.at[x, other], in_slab.at[x, me], x_send.at[x], x_recv.at[x],
                device_id={"dom": other}, device_id_type=MESH,
            ).start()
            return carry

        lax.fori_loop(0, dom_count - 1, one, 0, unroll=9)
        in_slab[x, me] = out_slab[x, me]

    def exchange_all(x):
        part = pl.ds(0, dom_count - 1)
        return pltpu.make_async_remote_copy(
            out_slab.at[x, part], in_slab.at[x, part], x_send.at[x], x_recv.at[x],
            device_id={"dom": lax.rem(me + 1, dom_count)}, device_id_type=MESH,
        )

    def wait_exchange(x):
        exchange_all(x).wait_recv()
        return from_slabs(in_slab[x])

    def shift(slot, src, dst, step):
        return pltpu.make_async_remote_copy(
            src, dst, sh_send.at[slot], sh_recv.at[slot],
            device_id={"phase": lax.rem(phase + step, phase_count)}, device_id_type=MESH,
        )

    sub_iota = lax.broadcasted_iota(jnp.int32, (TILE, TILE), 0)
    lane_iota = lax.broadcasted_iota(jnp.int32, (TILE, TILE), 1)

    slab_iota = lax.broadcasted_iota(jnp.int32, (TILE, dom_count), 0)
    dom_iota = lax.broadcasted_iota(jnp.int32, (TILE, dom_count), 1)
    in_slab_iota = lax.broadcasted_iota(jnp.int32, (TILE, 8), 0)
    cap_iota = lax.broadcasted_iota(jnp.int32, (TILE, 8), 1)
    lane_float = lane_iota.astype(F32)
    sub_float = sub_iota.astype(F32)
    mirror_high = lax.div(mirror[...], 8).astype(F32).astype(BF16)
    mirror_low = lax.rem(mirror[...], 8).astype(F32).astype(BF16)

    def build_want(b, carry):
        owner = (dom_iota == b * 16 + lax.div(slab_iota, 8)).astype(F32).astype(BF16)
        named = dot_nt(owner, mirror_high) * 8.0 + dot_nt(owner, mirror_low)
        named = jnp.where(cap_iota == lax.rem(in_slab_iota, 8), named, 0.0)
        col = jnp.broadcast_to(jnp.sum(named, axis=1, keepdims=True), (TILE, TILE))
        want_row[b] = jnp.transpose(col)[:8]
        for j in range(own_tiles):
            want_hot[rows_at(b, TILE), j * TILE:(j + 1) * TILE] = (col == lane_float + float(j * TILE)).astype(F32).astype(BF16)
        return carry

    lax.fori_loop(0, mirror_tiles, build_want, 0, unroll=True)

    def pick_rows(x, rows):
        out_slab[x] = to_slabs(dot(want_hot[...], rows))

    operand(0).wait()
    pick_rows(0, ns[...])
    pl.semaphore_wait(barrier, dom_count - 1 + 2)
    start_exchange(0)
    operand(1).wait()
    pick_rows(1, nf[...])
    start_exchange(1)

    def build_edges(b, carry):
        for end, hot, hot_t in ((0, send_hot, send_hot_t), (1, recv_hot, recv_hot_t)):
            row = jnp.broadcast_to(jnp.bitwise_and(ends[end:end + 1, rows_at(b, TILE)], TILE - 1), (TILE, TILE))
            hot_t[b] = (row == sub_iota).astype(F32).astype(BF16)
            hot[b] = (jnp.transpose(row) == lane_iota).astype(F32).astype(BF16)
        return carry

    lax.fori_loop(0, blocks, build_edges, 0)

    for j in range(mirror_tiles):
        row = jnp.broadcast_to(want_row[j, 0:1, :], (TILE, TILE))
        for i in range(own_tiles):
            want_hot_t[i * TILE:(i + 1) * TILE, j * TILE:(j + 1) * TILE] = (row == sub_float + float(i * TILE)).astype(F32).astype(BF16)

    table_s[0:own_tiles] = ns[...].reshape(own_tiles, TILE, features)
    table_f[0:own_tiles] = nf[...].reshape(own_tiles, TILE, features)

    def fetch(hot, b, table, end):
        return dot(hot[b], table[lax.div(s_ends[end, b * TILE], TILE)])

    def live_rows(i):
        at = lax.broadcasted_iota(jnp.int32, (EDGE_CHUNK, features), 0) + i * EDGE_CHUNK
        return jnp.where(at < cnt[0], 1.0, 0.0).astype(F32)

    def block_sum(hot_t, b, rows):
        high = rows.astype(BF16)
        low = (rows - high.astype(F32)).astype(BF16)
        return dot(jnp.concatenate([hot_t, hot_t], axis=1), jnp.concatenate([high, low], axis=0))

    def tile_total(k, first, count):
        total = jnp.zeros((TILE, features), F32)
        for b in range(count):
            end, block = divmod(first + b, blocks)
            tile = lax.div(ends[end:end + 1, block * TILE:block * TILE + 1], TILE)
            chosen = (tile == k).astype(F32)
            total = total + jnp.broadcast_to(chosen, (TILE, features)) * block_sums[b]
        return total

    def put_mirror_sums(x, first, count):
        def one(q, carry):
            total = tile_total(own_tiles + q, first, count)
            out_slab[x, pl.ds(pl.multiple_of(q * 16, 16), 16)] = to_slabs(total)
            return carry

        lax.fori_loop(0, mirror_tiles, one, 0, unroll=True)

    def own_sums(own, first, count):
        def one(k, carry):
            own[rows_at(k, TILE), :] = tile_total(k, first, count)
            return carry

        lax.fori_loop(0, own_tiles, one, 0)

    def edge_start(edges):
        edge_pre[...] = dot(edges[...], w1[:features, :]) + ev[0:1, :]

    def node_start(nodes):
        node_pre[...] = dot(nodes[...], nw1[:features, :]) + nv[0:1, :]

    def edge_forward(edges, table, keep):
        def one(i, carry):
            rows = rows_at(i, EDGE_CHUNK)
            from_send = jnp.concatenate(
                [fetch(send_hot, i * per_chunk + j, table, 0) for j in range(per_chunk)], axis=0
            ).astype(BF16)
            from_recv = jnp.concatenate(
                [fetch(recv_hot, i * per_chunk + j, table, 1) for j in range(per_chunk)], axis=0
            ).astype(BF16)
            stacked = jnp.concatenate([from_send, from_recv], axis=1)
            if keep:
                pre = edge_pre[rows, :] + dot(stacked, w1[features:, :])
            else:
                pre = dot(edges[rows, :], w1[:features, :]) + dot(stacked, w1[features:, :]) + ev[0:1, :]
            hidden = jnp.maximum(pre, 0.0).astype(BF16)
            normed, inverse = layer_norm(dot(hidden, w2[...]) + ev[1:2, :])
            message = live_rows(i) * (normed * ev[2:3, :] + ev[3:4, :])
            if keep:
                sent_rows[rows, :] = from_send
                recv_rows[rows, :] = from_recv
                edge_pre[rows, :] = pre
                edge_hid[rows, :] = hidden
                edge_norm[rows, :] = normed
                edge_inv[rows, :] = inverse
            else:
                new_edges[rows, :] = (edges[rows, :].astype(F32) + message).astype(BF16)
            for j in range(per_chunk):
                b = i * per_chunk + j
                block_sums[b] = block_sum(recv_hot_t[b], b, message[j * TILE:(j + 1) * TILE, :])
            return carry

        lax.fori_loop(0, edge_chunks, one, 0, unroll=UNROLL)

    def node_forward(nodes, own, returned, keep):
        def one(i, carry):
            rows = rows_at(i, NODE_CHUNK)
            total = own[rows, :] + dot(want_hot_t[rows, :], returned)
            gathered = total.astype(BF16)
            if keep:
                pre = node_pre[rows, :] + dot(gathered, nw1[features:, :])
            else:
                stacked = jnp.concatenate([nodes[rows, :], gathered], axis=1)
                pre = dot(stacked, nw1[...]) + nv[0:1, :]
            hidden = jnp.maximum(pre, 0.0).astype(BF16)
            normed, inverse = layer_norm(dot(hidden, nw2[...]) + nv[1:2, :])
            if keep:
                agg_rows[rows, :] = gathered
                node_pre[rows, :] = pre
                node_hid[rows, :] = hidden
                node_norm[rows, :] = normed
                node_inv[rows, :] = inverse
            else:
                new_nodes[rows, :] = (
                    nodes[rows, :].astype(F32) + (normed * nv[2:3, :] + nv[3:4, :])
                ).astype(BF16)
            return carry

        lax.fori_loop(0, node_chunks, one, 0, unroll=UNROLL)

    for n in (2, 3, 4, 5):
        operand(n).wait()
    edge_start(es)
    table_s[own_tiles:] = wait_exchange(0).reshape(mirror_tiles, TILE, features)
    edge_forward(es, table_s, True)
    put_mirror_sums(2, blocks, blocks)
    start_exchange(2)
    own_sums(own_s, blocks, blocks)

    operand(6).wait()
    table_f[own_tiles:] = wait_exchange(1).reshape(mirror_tiles, TILE, features)
    edge_forward(ef, table_f, False)
    shift(0, new_edges, o_ne, 1).start()
    put_mirror_sums(3, blocks, blocks)
    start_exchange(3)
    own_sums(own_f, blocks, blocks)

    for n in (7, 8, 9, 10):
        operand(n).wait()
    node_start(ns)
    returned = wait_exchange(2)
    node_forward(ns, own_s, returned, True)

    def node_back(i, carry):
        s_first, s_pre, s_gain, s_shift = carry
        rows = rows_at(i, NODE_CHUNK)
        top = nc[rows, :].astype(F32)
        normed = node_norm[rows, :]
        pre_grad = norm_back(top * nv[2:3, :], normed, node_inv[rows, :]).astype(BF16)
        first = jnp.where(node_pre[rows, :] > 0.0, dot_nt(pre_grad, nw2[...]), 0.0).astype(BF16)
        node_pre_grad[rows, :] = pre_grad
        node_first_grad[rows, :] = first
        table_g[rows_at(i, NODE_CHUNK // TILE)] = dot_nt(first, nw1[features:, :]).astype(BF16).reshape(NODE_CHUNK // TILE, TILE, features)
        return (
            s_first + col_sum(first.astype(F32)),
            s_pre + col_sum(pre_grad.astype(F32)),
            s_gain + col_sum(top * normed),
            s_shift + col_sum(top),
        )

    zero_row = jnp.zeros((1, features), F32)
    sums = lax.fori_loop(0, node_chunks, node_back, (zero_row,) * 4, unroll=UNROLL)
    for j in range(4):
        vec[4 + j:5 + j, :] = sums[j]

    pick_rows(4, table_g[0:own_tiles].reshape(node_dev, features))
    start_exchange(4)

    def start_a(which, grads, arrived, used):
        arrived[apos] = grads[apos]
        for k in A_ORDER:
            other, device = a_partner(k)
            pltpu.make_async_remote_copy(
                grads.at[other, pl.ds(0, used)], arrived.at[apos, pl.ds(0, used)],
                ra_s.at[which], ra_r.at[which], device_id={"dom": device}, device_id_type=MESH,
            ).start()

    def all_a(which, grads, arrived, used):
        part = pl.ds(0, GROUP - 1)
        return pltpu.make_async_remote_copy(
            grads.at[part, pl.ds(0, used)], arrived.at[part, pl.ds(0, used)],
            ra_s.at[which], ra_r.at[which], device_id={"dom": a_partner(1)[1]}, device_id_type=MESH,
        )

    def start_b(which, arrived):
        total = arrived[0].astype(F32)
        for k in range(1, GROUP):
            total = total + arrived[k].astype(F32)
        sb[which] = total.astype(BF16).reshape(Z_SIZE, 16, features)
        rb[which, zpos] = sb[which, zpos]
        for k in B_ORDER:
            other, device = b_partner(k)
            pltpu.make_async_remote_copy(
                sb.at[which, other], rb.at[which, zpos], rb_s.at[which], rb_r.at[which],
                device_id={"dom": device}, device_id_type=MESH,
            ).start()

    def all_b(which):
        part = pl.ds(0, Z_SIZE - 1)
        return pltpu.make_async_remote_copy(
            sb.at[which, part], rb.at[which, part], rb_s.at[which], rb_r.at[which],
            device_id={"dom": b_partner(1)[1]}, device_id_type=MESH,
        )

    def start_gather_b(which):
        total = rb[which, 0].astype(F32)
        for k in range(1, Z_SIZE):
            total = total + rb[which, k].astype(F32)
        fb[which] = total.astype(BF16)
        ab[which, zpos] = fb[which]
        for k in B_ORDER:
            other, device = b_partner(k)
            pltpu.make_async_remote_copy(
                fb.at[which], ab.at[which, zpos], gb_s.at[which], gb_r.at[which],
                device_id={"dom": device}, device_id_type=MESH,
            ).start()

    def all_gather_b(which):
        part = pl.ds(0, Z_SIZE - 1)
        return pltpu.make_async_remote_copy(
            ab.at[which, part], ab.at[which, part], gb_s.at[which], gb_r.at[which],
            device_id={"dom": b_partner(1)[1]}, device_id_type=MESH,
        )

    z_used = ((3 * features) // GROUP // 16, Z_SIZE)

    def own_share(which, out):
        part = pl.ds(0, z_used[which])
        return pltpu.make_async_copy(ab.at[which, part], out.at[apos, part], local_sem.at[which])

    def start_gather_a(which, out):
        part = pl.ds(0, z_used[which])
        own_share(which, out).start()
        for k in A_ORDER:
            other, device = a_partner(k)
            pltpu.make_async_remote_copy(
                ab.at[which, part], out.at[apos, part], ga_s.at[which], ga_r.at[which],
                device_id={"dom": device}, device_id_type=MESH,
            ).start()

    def all_gather_a(which, out):
        part = pl.ds(0, GROUP - 1)
        used = pl.ds(0, z_used[which])
        return pltpu.make_async_remote_copy(
            out.at[part, used], out.at[part, used], ga_s.at[which], ga_r.at[which],
            device_id={"dom": a_partner(1)[1]}, device_id_type=MESH,
        )

    node_used = (3 * features) // GROUP

    def put_node_grads(first_row, grad):
        at = 0
        while at < grad.shape[0]:
            share, inner = divmod(first_row + at, node_used)
            size = min(node_used - inner, grad.shape[0] - at)
            g_node[share, inner:inner + size, :] = grad[at:at + size, :].astype(BF16)
            at += size

    for j in range(GROUP):
        g_node[j, node_used:, :] = jnp.zeros((TILE - node_used, features), BF16)
        ra_node[j, node_used:, :] = jnp.zeros((TILE - node_used, features), BF16)
    put_node_grads(0, dot_tn(ns[...], node_first_grad[...]))
    put_node_grads(features, dot_tn(agg_rows[...], node_first_grad[...]))
    put_node_grads(2 * features, dot_tn(node_hid[...], node_pre_grad[...]))
    start_a(0, g_node, ra_node, node_used)

    def node_base(i, carry):
        rows = rows_at(i, NODE_CHUNK)
        base[rows, :] = nc[rows, :].astype(F32) + dot_nt(node_first_grad[rows, :], nw1[:features, :])
        return carry

    lax.fori_loop(0, node_chunks, node_base, 0, unroll=UNROLL)

    node_forward(nf, own_f, wait_exchange(3), False)
    shift(1, new_nodes, o_nn, 1).start()

    all_a(0, g_node, ra_node, node_used).wait_recv()
    start_b(0, ra_node)

    operand(11).wait()
    table_g[own_tiles:] = wait_exchange(4).reshape(mirror_tiles, TILE, features)

    def edge_back(i, carry):
        s_first, s_pre, s_gain, s_shift = carry
        rows = rows_at(i, EDGE_CHUNK)
        from_recv = jnp.concatenate(
            [fetch(recv_hot, i * per_chunk + j, table_g, 1) for j in range(per_chunk)], axis=0
        )
        top = live_rows(i) * (ec[rows, :].astype(F32) + from_recv)
        normed = edge_norm[rows, :]
        pre_grad = norm_back(top * ev[2:3, :], normed, edge_inv[rows, :]).astype(BF16)
        first = jnp.where(edge_pre[rows, :] > 0.0, dot_nt(pre_grad, w2[...]), 0.0).astype(BF16)
        edge_pre_grad[rows, :] = pre_grad
        edge_first_grad[rows, :] = first
        to_send = dot_nt(first, w1[features:2 * features, :])
        to_recv = dot_nt(first, w1[2 * features:, :])
        for j in range(per_chunk):
            b = i * per_chunk + j
            block_sums[b] = block_sum(send_hot_t[b], b, to_send[j * TILE:(j + 1) * TILE, :])
            block_sums[blocks + b] = block_sum(recv_hot_t[b], b, to_recv[j * TILE:(j + 1) * TILE, :])
        return (
            s_first + col_sum(first.astype(F32)),
            s_pre + col_sum(pre_grad.astype(F32)),
            s_gain + col_sum(top * normed),
            s_shift + col_sum(top),
        )

    sums = lax.fori_loop(0, edge_chunks, edge_back, (zero_row,) * 4, unroll=UNROLL)
    for j in range(4):
        vec[j:j + 1, :] = sums[j]
    for part, rows in enumerate((es, sent_rows, recv_rows)):
        grad = dot_tn(rows[...], edge_first_grad[...]).astype(BF16)
        g_edge[2 * part] = grad[:TILE, :]
        g_edge[2 * part + 1] = grad[TILE:, :]
    grad = dot_tn(edge_hid[...], edge_pre_grad[...]).astype(BF16)
    g_edge[6] = grad[:TILE, :]
    g_edge[7] = grad[TILE:, :]
    start_a(1, g_edge, ra_edge, TILE)

    put_mirror_sums(5, 0, 2 * blocks)
    start_exchange(5)

    def edge_out(i, carry):
        rows = rows_at(i, EDGE_CHUNK)
        old_edges[rows, :] = (
            ec[rows, :].astype(F32) + dot_nt(edge_first_grad[rows, :], w1[:features, :])
        ).astype(BF16)
        return carry

    lax.fori_loop(0, edge_chunks, edge_out, 0, unroll=UNROLL)
    shift(2, old_edges, o_pe, phase_count - 1).start()

    all_b(0).wait_recv()
    start_gather_b(0)

    va[apos] = vec[...]
    for k in range(1, GROUP):
        other, device = a_partner(k)
        pltpu.make_async_remote_copy(
            vec, va.at[apos], v_s.at[0], v_r.at[0], device_id={"dom": device}, device_id_type=MESH
        ).start()

    own_sums(own_s, 0, 2 * blocks)
    all_a(1, g_edge, ra_edge, TILE).wait_recv()
    start_b(1, ra_edge)
    all_gather_b(0).wait_recv()
    start_gather_a(0, o_gn)

    returned = wait_exchange(5)

    for i in range(node_dev // OUT_CHUNK):
        rows = pl.ds(i * OUT_CHUNK, OUT_CHUNK)
        old_nodes[rows, :] = (base[rows, :] + own_s[rows, :] + dot(want_hot_t[rows, :], returned)).astype(BF16)
        shift(3, old_nodes.at[rows, :], o_pn.at[rows, :], phase_count - 1).start()

    all_b(1).wait_recv()
    start_gather_b(1)
    group_part = pl.ds(0, GROUP - 1)
    first_all = pltpu.make_async_remote_copy(
        va.at[group_part], va.at[group_part], v_s.at[0], v_r.at[0],
        device_id={"dom": a_partner(1)[1]}, device_id_type=MESH,
    )
    first_all.wait_recv()
    first_all.wait_send()
    total = va[0]
    for k in range(1, GROUP):
        total = total + va[k]
    vec[...] = total
    vb[zpos] = total
    for k in range(1, Z_SIZE):
        other, device = b_partner(k)
        pltpu.make_async_remote_copy(
            vec, vb.at[zpos], v_s.at[1], v_r.at[1], device_id={"dom": device}, device_id_type=MESH
        ).start()

    all_gather_b(1).wait_recv()
    start_gather_a(1, o_ge)
    second_all = pltpu.make_async_remote_copy(
        vb.at[group_part], vb.at[group_part], v_s.at[1], v_r.at[1],
        device_id={"dom": b_partner(1)[1]}, device_id_type=MESH,
    )
    second_all.wait_recv()
    total = vb[0]
    for k in range(1, Z_SIZE):
        total = total + vb[k]
    o_gv[...] = total

    for x in range(6):
        exchange_all(x).wait_send()
    all_a(0, g_node, ra_node, node_used).wait_send()
    all_a(1, g_edge, ra_edge, TILE).wait_send()
    second_all.wait_send()
    for which, out in ((0, o_gn), (1, o_ge)):
        all_b(which).wait_send()
        all_gather_b(which).wait_send()
        own_share(which, out).wait()
        all_gather_a(which, out).wait_send()
        all_gather_a(which, out).wait_recv()
    shift(0, new_edges, o_ne, 1).wait()
    shift(1, new_nodes, o_nn, 1).wait()
    shift(2, old_edges, o_pe, phase_count - 1).wait()
    shift(3, old_nodes, o_pn, phase_count - 1).wait()


def tick(dom_count, phase_count, *arrays):
    edge_dev, features = arrays[0].shape
    node_dev = arrays[1].shape[0]
    blocks = edge_dev // TILE
    slots = node_dev + dom_count * 8
    vmem = lambda shape, kind=BF16: pltpu.VMEM(shape, kind)
    sem = lambda count: pltpu.SemaphoreType.DMA((count,))
    mirror_tiles = dom_count * 8 // TILE
    scratch = (
        [vmem(a.shape, a.dtype) for a in arrays[:12]]
        + [vmem((mirror_tiles, 8, TILE), F32)]
        + [vmem((blocks, TILE, TILE))] * 4
        + [vmem((dom_count * 8, node_dev)), vmem((node_dev, dom_count * 8))]
        + [vmem((slots // TILE, TILE, features))] * 3
        + [vmem((6, dom_count, 16, 128))] * 2
        + [vmem((edge_dev, features))] * 2
        + [vmem((edge_dev, features), F32), vmem((edge_dev, features)), vmem((edge_dev, features), F32), vmem((edge_dev, 1), F32)]
        + [vmem((edge_dev, features))] * 2
        + [vmem((node_dev, features), F32), vmem((node_dev, features)), vmem((node_dev, features), F32), vmem((node_dev, 1), F32)]
        + [vmem((node_dev, features))] * 3
        + [vmem((2 * blocks, TILE, features), F32)]
        + [vmem((node_dev, features), F32)] * 3
        + [vmem((edge_dev, features)), vmem((node_dev, features))] * 2
        + [vmem((GROUP, TILE, features))] * 4
        + [vmem((2, Z_SIZE, 16, features))] * 2
        + [vmem((2, 16, features)), vmem((2, Z_SIZE, 16, features))]
        + [vmem((GROUP, 8, features), F32), vmem((Z_SIZE, 8, features), F32), vmem((8, features), F32)]
        + [sem(6), sem(6), sem(4), sem(4)]
        + [sem(2)] * 11
        + [sem(12)]
    )
    in_hbm = pl.BlockSpec(memory_space=pltpu.HBM)
    in_vmem = pl.BlockSpec(memory_space=pltpu.VMEM)
    in_smem = pl.BlockSpec(memory_space=pltpu.SMEM)
    anywhere = pl.BlockSpec(memory_space=pl.ANY)
    out_shape = (
        jax.ShapeDtypeStruct((edge_dev, features), BF16),
        jax.ShapeDtypeStruct((node_dev, features), BF16),
        jax.ShapeDtypeStruct((edge_dev, features), BF16),
        jax.ShapeDtypeStruct((node_dev, features), BF16),
        jax.ShapeDtypeStruct((GROUP, Z_SIZE, 16, features), BF16),
        jax.ShapeDtypeStruct((GROUP, Z_SIZE, 16, features), BF16),
        jax.ShapeDtypeStruct((8, features), F32),
    )

    def kernel(*refs):
        tick_kernel(dom_count, phase_count, *refs)

    return pl.pallas_call(
        kernel,
        out_shape=out_shape,
        in_specs=[in_hbm] * 12 + [in_vmem] * 2 + [in_smem] * 2,
        out_specs=[anywhere] * 6 + [in_vmem],
        scratch_shapes=scratch,
        name="tick",
        compiler_params=pltpu.CompilerParams(
            collective_id=0, has_side_effects=True, vmem_limit_bytes=VMEM_BYTES
        ),
    )(*arrays)


def hand_over_kernel(
    ne, nn, pe, pn, ge, gn, gv,
    o_ne, o_nn, o_pe, o_pn, o_ew1, o_ew2, o_ev, o_nw1, o_nw2, o_nv,
    ew1, ew2, nw1, nw2, v_ne, v_nn, v_pe, v_pn, v_ge, v_gn, v_gv, in_sems, sems,
):
    features = gv.shape[1]
    arriving = [(gn, v_gn), (ge, v_ge), (gv, v_gv), (ne, v_ne), (nn, v_nn), (pe, v_pe), (pn, v_pn)]
    arriving = [pltpu.make_async_copy(src, dst, in_sems.at[n]) for n, (src, dst) in enumerate(arriving)]
    copies = [(v_ne, o_ne.at[0]), (v_nn, o_nn.at[0]), (v_pe, o_pe.at[0]), (v_pn, o_pn.at[0])]
    copies += [(v_gv.at[pl.ds(0, 4)], o_ev.at[0]), (v_gv.at[pl.ds(4, 4)], o_nv.at[0])]
    copies += [(ew1, o_ew1.at[0]), (ew2, o_ew2.at[0]), (nw1, o_nw1.at[0]), (nw2, o_nw2.at[0])]
    copies = [pltpu.make_async_copy(src, dst, sems.at[n]) for n, (src, dst) in enumerate(copies)]
    for copy in arriving:
        copy.start()
    arriving[0].wait()
    used = (3 * features) // GROUP
    cut = 2 * features
    for share in range(GROUP):
        rows = v_gn[share, 0:used // 16].reshape(used, features).astype(F32)
        first = share * used
        inner = min(max(cut - first, 0), used)
        if inner > 0:
            nw1[first:first + inner, :] = rows[:inner]
        if inner < used:
            nw2[first + inner - cut:first + used - cut, :] = rows[inner:]
    copies[8].start()
    copies[9].start()
    arriving[1].wait()
    ew1[...] = v_ge[0:6].reshape(3 * features, features).astype(F32)
    copies[6].start()
    ew2[...] = v_ge[6:8].reshape(features, features).astype(F32)
    copies[7].start()
    arriving[2].wait()
    copies[4].start()
    copies[5].start()
    for n in range(4):
        arriving[3 + n].wait()
        copies[n].start()
    for copy in copies:
        copy.wait()


def hand_over(ne, nn, pe, pn, ge, gn, gv):
    features = gv.shape[1]
    shape = lambda rows, kind: jax.ShapeDtypeStruct((1, rows, features), kind)
    out_shape = tuple(shape(a.shape[0], BF16) for a in (ne, nn, pe, pn)) + (
        shape(3 * features, F32), shape(features, F32), shape(4, F32),
        shape(2 * features, F32), shape(features, F32), shape(4, F32),
    )
    grads = [pltpu.VMEM((n * features, features), F32) for n in (3, 1, 2, 1)]
    held = [pltpu.VMEM(a.shape, a.dtype) for a in (ne, nn, pe, pn, ge, gn, gv)]
    in_hbm = pl.BlockSpec(memory_space=pltpu.HBM)
    return pl.pallas_call(
        hand_over_kernel,
        out_shape=out_shape,
        in_specs=[in_hbm] * 7,
        out_specs=[in_hbm] * 10,
        scratch_shapes=grads + held + [pltpu.SemaphoreType.DMA((7,)), pltpu.SemaphoreType.DMA((10,))],
        name="hand_over",
        compiler_params=pltpu.CompilerParams(vmem_limit_bytes=VMEM_BYTES),
    )(ne, nn, pe, pn, ge, gn, gv)


def on_device(
    edges_fwd, nodes_fwd, edges_stash, nodes_stash, edge_cot, node_cot,
    edge_w1, edge_w2, edge_vectors, node_w1, node_w2, node_vectors,
    edge_nodes, mirror_rows, edge_count,
):
    dom_count = lax.axis_size("dom")
    phase_count = lax.axis_size("phase")
    features = edges_fwd.shape[2]
    ne, nn, pe, pn, ge, gn, gv = tick(
        dom_count, phase_count,
        edges_fwd[0], nodes_fwd[0], edges_stash[0], nodes_stash[0], edge_cot[0], node_cot[0],
        edge_w1[0], edge_w2[0], edge_vectors[0], node_w1[0], node_w2[0], node_vectors[0],
        edge_nodes, mirror_rows[0].T, edge_nodes, edge_count,
    )
    return hand_over(ne, nn, pe, pn, ge, gn, gv)


def solution(mesh):
    rows = P("phase", "dom", None)
    whole = P("phase", None, None)
    in_specs = (rows,) * 6 + (whole,) * 6 + (P(None, "dom"), P("dom", None, None), P("dom"))
    out_specs = (rows,) * 4 + (whole,) * 6
    return jax.shard_map(
        on_device, mesh=mesh, in_specs=in_specs, out_specs=out_specs, check_vma=False
    )
```
